128 devices in a mesh: agent: 8 (over z, core), cluster: 16 (over x, y).
Axes of the slice: x: 4, y: 4, z: 4, core: 2. Of those that a mesh axis runs over, the one named last changes fastest.
Arguments:
- jacobians: bfloat16 [72, 65536], P(None, ('agent', 'cluster')), may hold values from -6 to 6
- point_hessians: float32 [6, 65536], P(None, ('agent', 'cluster')), as said below
- cameras: int32 [4, 65536], P(None, ('agent', 'cluster')), may hold values from 0 to 255, as said below
- tiles: int32 [65536], P(('agent', 'cluster')), may hold values from 0 to 127, as said below
- damping: int32 [8], replicated, may hold values from 1 to 16
Outputs:
- band: float32 [12288, 24576], P('agent', 'cluster')
The draws below stay inside these ranges and needn't reach their ends.
Inputs may be any that keep to these rules, and one draw needn't show every extreme that they name: `point_hessians`: the point block of every track is symmetric positive definite; each off-diagonal entry is at most 0.45 times the square root of the product of its two diagonal entries, and the diagonal entries are positive. The 4 cameras of one track are distinct. `tiles`: among the 512 tracks of one device (aligned blocks of the array) at most 12 feed one tile; one tile is fed by exactly 12 tracks of every device.
All inputs are finite; a program needn't handle non-finite values.
Results may differ from the reference program's by a relative error of at most 0.00086.
Values may be sent and summed in bfloat16 or wider, within the bound.
A program may use at most 256 MiB of HBM per device.

```python
import jax
import jax.numpy as jnp
from jax import lax

CAMS = 256
OBS = 4
TRK_DEV = 512
CAP = 12
TRACKS = 65536
N_AGENT = 8
N_CLUSTER = 16


def draw_point_hessians(key, part):
    key = jax.random.fold_in(key, 11)
    key_diag, key_off = jax.random.split(key)
    count = TRK_DEV * N_AGENT * N_CLUSTER
    diag = jax.random.uniform(key_diag, (3, count), jnp.float32, 2.0, 6.0)
    pairs = jnp.stack([diag[0] * diag[1], diag[0] * diag[2], diag[1] * diag[2]])
    off = jax.random.uniform(key_off, (3, count), jnp.float32, -0.45, 0.45) * jnp.sqrt(pairs)
    return jnp.concatenate([diag, off], axis=0).astype(jnp.float32)


def draw_cameras(key, part):
    key = jax.random.fold_in(key, 12)
    key_start, key_gap = jax.random.split(key)
    count = TRK_DEV * N_AGENT * N_CLUSTER
    start = jax.random.randint(key_start, (1, count), 0, CAMS)
    gaps = jax.random.randint(key_gap, (OBS - 1, count), 1, CAMS // 4 + 1)
    offsets = jnp.concatenate([jnp.zeros((1, count), jnp.int32), jnp.cumsum(gaps, axis=0)], axis=0)
    return ((start + offsets) % CAMS).astype(jnp.int32)


def draw_tiles(key, part):
    key = jax.random.fold_in(key, 13)
    grid = N_AGENT * N_CLUSTER
    heavy = jax.random.randint(jax.random.fold_in(key, 0), (), 0, grid)
    table = jnp.arange((grid - 1) * CAP, dtype=jnp.int32) // CAP
    table = table + (table >= heavy).astype(jnp.int32)

    def one_device(dev_key):
        key_pick, key_order = jax.random.split(dev_key)
        picked = jax.random.permutation(key_pick, table)[:TRK_DEV - CAP]
        merged = jnp.concatenate([picked, jnp.full((CAP,), heavy, jnp.int32)])
        return jax.random.permutation(key_order, merged)
    dev_keys = jax.random.split(jax.random.fold_in(key, 1), grid)
    return jax.vmap(one_device)(dev_keys).reshape(-1).astype(jnp.int32)


def place_ends(entries, rng, low, high):
    shape = entries.shape
    spot = [jax.random.randint(jax.random.fold_in(rng, axis), (), 0, shape[axis]) for axis in range(len(shape))]
    entries = entries.at[tuple(spot)].set(low)
    longest = shape.index(max(shape))
    spot[longest] = (spot[longest] + 1) % shape[longest]
    return entries.at[tuple(spot)].set(high)


def levels(rng, dims, pieces, low, largest):
    level, own = 1.0, jax.random.fold_in(rng, 6)
    for axis_at, blocks in pieces:
        steps = jnp.exp(jax.random.uniform(jax.random.fold_in(own, axis_at), (blocks,), jnp.float32, low / len(pieces), largest / len(pieces)))
        level = level * jnp.repeat(steps, dims[axis_at] // blocks).reshape([-1 if axis == axis_at else 1 for axis in range(len(dims))])
    return level


def normal_values(stream_key, dims, scale, limit, cuts=(), held_as=jnp.bfloat16):
    array = scale * jax.random.normal(stream_key, dims, jnp.float32)
    if cuts:
        array = array * levels(stream_key, dims, cuts, -0.22, 0.18)
    return jnp.clip(array, -limit, limit).astype(held_as)


def setup_inputs(seed: int = 0) -> dict:
    seeds = jax.random.split(jax.random.key(seed), 6)
    return {
        "jacobians": normal_values(seeds[0], (18 * OBS, TRACKS), 1.0, 6.0, ((1, 128),)),
        "point_hessians": draw_point_hessians(jax.random.fold_in(seeds[5], 71), 0),
        "cameras": draw_cameras(jax.random.fold_in(seeds[5], 71), 0),
        "tiles": draw_tiles(jax.random.fold_in(seeds[5], 71), 0),
        "damping": place_ends(jax.random.randint(seeds[4], (N_AGENT,), 1, 17), jax.random.fold_in(seeds[4], 1), 1, 16).astype(jnp.int32),
    }


def point_inverse(hess):
    a, b, c, d, e, f = (hess[0], hess[1], hess[2], hess[3], hess[4], hess[5])
    c00 = b * c - f * f
    c11 = a * c - e * e
    c22 = a * b - d * d
    c01 = e * f - d * c
    c02 = d * f - e * b
    c12 = d * e - a * f
    det = a * c00 + d * c01 + e * c02
    rows = jnp.stack([jnp.stack([c00, c01, c02]), jnp.stack([c01, c11, c12]), jnp.stack([c02, c12, c22])])
    return rows / det

def reference(jacobians, point_hessians, cameras, tiles, damping):
    count = tiles.shape[0]
    order = 6 * CAMS
    pinv = point_inverse(point_hessians)
    jac = jacobians.astype(jnp.float32).reshape(OBS, 6, 3, count)
    weighted = jnp.einsum('oris,ijs->orjs', jac, pinv, precision=lax.Precision.HIGHEST).astype(jnp.bfloat16)
    weighted = lax.optimization_barrier(weighted).astype(jnp.float32)
    row_of = tiles // N_CLUSTER
    col_of = tiles % N_CLUSTER
    on_diag = row_of == col_of
    obs_idx = jnp.arange(OBS, dtype=jnp.int32)[:, None]
    left = jnp.logical_or(on_diag[None, :], obs_idx < 2).astype(jnp.float32)
    right = jnp.logical_or(on_diag[None, :], obs_idx >= 2).astype(jnp.float32)
    blocks = jnp.einsum('aris,bqis,as,bs->abrqs', weighted, jac, left, right, precision=lax.Precision.HIGHEST)
    six = jnp.arange(6, dtype=jnp.int32)
    row_idx = 6 * cameras[:, None, None, None, :] + six[None, None, :, None, None]
    col_idx = 6 * cameras[None, :, None, None, :] + six[None, None, None, :, None]
    flat = tiles[None, None, None, None, :] * (order * order) + row_idx * order + col_idx
    flat = jnp.broadcast_to(flat, blocks.shape).astype(jnp.int32)
    big = jnp.zeros((N_AGENT * N_CLUSTER * order * order,), jnp.float32)
    big = big.at[flat.ravel()].add(blocks.ravel())
    big = big.reshape(N_AGENT, N_CLUSTER, order, order)
    rows_out = []
    for brow in range(N_AGENT):
        own = big[brow, brow]
        scale = damping[brow].astype(jnp.float32) / 8.0
        damped = own + scale * jnp.diag(jnp.diagonal(own) + 1.0)
        lower = jnp.linalg.cholesky(damped)
        whole = jnp.concatenate([big[brow, col] for col in range(N_CLUSTER)], axis=1)
        solved = jax.scipy.linalg.solve_triangular(lower, whole, lower=True)
        solved = solved.at[:, brow * order:(brow + 1) * order].set(lower)
        rows_out.append(solved)
    return jnp.concatenate(rows_out, axis=0)
```

```python
import functools

import jax
import jax.numpy as jnp
import numpy as np
from jax import lax
from jax.experimental import pallas as pl
from jax.experimental.pallas import tpu as pltpu
from jax.sharding import PartitionSpec as P

F32 = jnp.float32
BF16 = jnp.bfloat16
CAMS = 256
OBS = 4
ORDER = 6 * CAMS
ROOM = 12
PAIR = 2 * ROOM
FEAT = 128
CHUNK = 256
NB = 128
SUB = 16


def iota(shape, dim):
    return lax.broadcasted_iota(jnp.int32, shape, dim)


def dot_t(left, right):
    return lax.dot_general(left, right, (((1,), (1,)), ((), ())), preferred_element_type=F32)


def dot(left, right):
    return jnp.dot(left, right, preferred_element_type=F32)


def split(x):
    high = x.astype(BF16)
    return high, (x - high.astype(F32)).astype(BF16)


def pack_kernel(agents, clusters, jac_ref, hess_ref, cam_ref, tile_ref, out_ref, feat):
    devices = agents * clusters
    local = tile_ref.shape[1]
    tiles = tile_ref[...]
    hot = iota((devices, local), 0) == tiles
    tri = (iota((local, local), 0) <= iota((local, local), 1)).astype(F32).astype(BF16)
    count = dot(hot.astype(F32).astype(BF16), tri)
    rank = jnp.sum(jnp.where(hot, count, 0.0), axis=0, keepdims=True) - 1.0
    key = tiles * 16 + rank.astype(jnp.int32)
    hess = hess_ref[...]
    high = hess.astype(BF16).astype(F32)
    rest = hess - high
    mid = rest.astype(BF16).astype(F32)
    feat[...] = jnp.zeros_like(feat)
    feat[0:72, :] = jac_ref[...].astype(F32)
    feat[72:78, :] = high
    feat[80:86, :] = mid
    feat[88:94, :] = rest - mid
    feat[96:100, :] = cam_ref[...].astype(F32)
    feat[100:101, :] = jnp.ones((1, local), F32)
    feats = feat[...].astype(BF16)
    slot = iota((PAIR, local), 0)
    own = slot < ROOM
    rows = clusters * PAIR

    def agent(b, carry):
        parts = []
        for d in range(clusters):
            want = jnp.where(own, (b * clusters + d) * 16 + slot, (b * clusters + b) * 16 + slot - ROOM)
            parts.append(jnp.where(want == key, 1.0, 0.0).astype(F32))
        pick = jnp.concatenate(parts, axis=0).astype(BF16)
        out_ref[pl.ds(pl.multiple_of(b * rows, rows), rows), :] = dot_t(pick, feats).astype(BF16)
        return carry

    lax.fori_loop(0, agents, agent, 0)


def factor_inverse(block, cols, rows16):
    nb = SUB
    lane = iota((nb, NB), 1)
    sub = iota((nb, NB), 0)
    lane_all = iota((NB, NB), 1)
    for k in range(NB // nb):
        o = nb * k
        x = block[o : o + nb, :]
        for j in range(nb):
            cols[j] = jnp.broadcast_to(x[:, o + j : o + j + 1], (nb, NB))
        inside = (lane >= o) & (lane < o + nb)
        rows16[...] = jnp.where(inside, jnp.where(lane - o == sub, 1.0, 0.0).astype(F32), x)
        s = [[None] * nb for _ in range(nb)]
        for j in range(nb):
            for i in range(j, nb):
                s[i][j] = jnp.broadcast_to(cols[j, i : i + 1, :], (8, NB))
        rows = [jnp.broadcast_to(rows16[i : i + 1, :], (8, NB)) for i in range(nb)]
        for j in range(nb):
            root = lax.rsqrt(s[j][j])
            rows[j] = rows[j] * root
            low = [None] * nb
            for i in range(j + 1, nb):
                low[i] = s[i][j] * root
            for i in range(j + 1, nb):
                for q in range(j + 1, i + 1):
                    s[i][q] = s[i][q] - low[i] * low[q]
                rows[i] = rows[i] - low[i] * rows[j]
        for i in range(nb):
            rows16[i : i + 1, :] = rows[i][0:1, :]
        done = rows16[...]
        kept = jnp.where((lane_all >= o) & (lane_all < o + nb), 0.0, block[...])
        if k < NB // nb - 1:
            high, low_part = split(done)
            left_high, left_low = split(jnp.where(lane >= o + nb, done, 0.0))
            left = jnp.concatenate([left_high, left_high, left_low], axis=0)
            right = jnp.concatenate([high, low_part, high], axis=0)
            kept = kept - lax.dot_general(left, right, (((0,), (0,)), ((), ())), preferred_element_type=F32)
        block[...] = kept
        block[o : o + nb, :] = done


def slots_of(recv_ref, source_ref, before_ref, place_ref):
    total = recv_ref.shape[0]
    sources = total // PAIR
    flag = jnp.where(iota((8, FEAT), 1) == 100, 1.0, 0.0).astype(F32).astype(BF16)
    valid = dot_t(flag, recv_ref[...])
    lane = iota((8, total), 1).astype(F32)
    source = jnp.floor((lane + 0.5) * (1.0 / PAIR))
    slot = lane - source * PAIR
    home = iota((sources, total), 0).astype(F32)
    source_row = jnp.broadcast_to(source[0:1, :], (sources, total))
    source_ref[...] = jnp.where(home == source_row, 1.0, 0.0).astype(F32).astype(BF16)
    before_ref[...] = jnp.where(home < source_row, 1.0, 0.0).astype(F32).astype(BF16)
    counts = []
    for part in range(2):
        mine = (slot < ROOM) if part == 0 else (slot >= ROOM)
        here = jnp.where(mine, valid, 0.0)
        per_source = dot_t(here.astype(BF16), source_ref[...])
        offset = dot(per_source.astype(BF16), before_ref[...])
        place = jnp.where(here > 0.5, offset + slot - part * ROOM, -1.0)
        place_ref[part : part + 1, :] = place[0:1, :].astype(jnp.int32)
        counts.append(jnp.sum(here[0:1, :]).astype(jnp.int32))
    return counts


def assemble(diagonal, part, count, recv_ref, place_ref, order_ref, spread_ref, left, right, target):
    target[...] = jnp.zeros_like(target)
    total = recv_ref.shape[0]
    left_obs = range(OBS) if diagonal else (0, 1)
    right_obs = range(OBS) if diagonal else (2, 3)

    def chunk(at, carry):
        want = iota((CHUNK, total), 0) + at * CHUNK
        pick = jnp.where(want == place_ref[part : part + 1, :], 1.0, 0.0).astype(F32).astype(BF16)
        tracks = dot(pick, recv_ref[...]).astype(BF16)
        x = dot_t(order_ref[...], tracks)
        h = x[72:80, :] + x[80:88, :] + x[88:96, :]
        a, b, c, d, e, f = (h[q : q + 1, :] for q in range(6))
        c00 = b * c - f * f
        c11 = a * c - e * e
        c22 = a * b - d * d
        c01 = e * f - d * c
        c02 = d * f - e * b
        c12 = d * e - a * f
        det = a * c00 + d * c01 + e * c02
        det = jnp.where(x[100:101, :] > 0.5, det, 1.0)
        inv = [[c00 / det, c01 / det, c02 / det], [c01 / det, c11 / det, c12 / det], [c02 / det, c12 / det, c22 / det]]
        jac = [x[24 * i : 24 * i + 24, :] for i in range(3)]
        wide_j, wide_w = [], []
        for j in range(3):
            w = jac[0] * inv[0][j] + jac[1] * inv[1][j] + jac[2] * inv[2][j]
            wide_w.append(dot(spread_ref[...], w.astype(BF16)).astype(BF16))
            wide_j.append(dot(spread_ref[...], jac[j].astype(BF16)).astype(BF16))
        cams = [jnp.broadcast_to(x[96 + o : 97 + o, :].astype(BF16), (48, CHUNK)) for o in range(OBS)]
        local_cam = jnp.floor((iota((48, CHUNK), 0).astype(F32) + 0.5) * (1.0 / 6.0))

        def rows(q, carry):
            cam = (local_cam + (8 * q).astype(F32)).astype(BF16)
            at_row = pl.ds(pl.multiple_of(q * 48, 48), 48)
            hits = [cam == cams[o] for o in range(OBS)]
            for j in range(3):
                at_col = slice(CHUNK * j, CHUNK * (j + 1))
                for obs, wide, out in ((left_obs, wide_w[j], left), (right_obs, wide_j[j], right)):
                    value = jnp.zeros((48, CHUNK), BF16)
                    for o in obs:
                        value = jnp.where(hits[o], wide[48 * o : 48 * o + 48, :], value)
                    out[at_row, at_col] = value
            return carry

        lax.fori_loop(0, ORDER // 48, rows, 0)
        step = 256
        for m in range(ORDER // step):
            at_row = slice(step * m, step * (m + 1))
            if diagonal:
                upto = slice(0, step * (m + 1))
                both = dot_t(left[at_row, :], right[upto, :]) + dot_t(right[at_row, :], left[upto, :])
                target[at_row, upto] += 0.5 * both
            else:
                target[at_row, :] += dot_t(left[at_row, :], right[...])
        return carry

    lax.fori_loop(0, (count + CHUNK - 1) // CHUNK, chunk, 0)


def solve_kernel(
    place_at, recv_ref, order_ref, spread_ref, out_ref,
    system, left, right, source, before, place, block, cols, rows16, low1, low2, wide,
):
    b, d, damp = place_at[0], place_at[1], place_at[2]
    on_diag = b == d
    own_count, diag_count = slots_of(recv_ref, source, before, place)
    own_count = jnp.where(on_diag, 0, own_count)
    assemble(False, 0, own_count, recv_ref, place, order_ref, spread_ref, left, right, out_ref)
    assemble(True, 1, diag_count, recv_ref, place, order_ref, spread_ref, left, right, system)
    scale = damp.astype(F32) / 8.0
    eye = iota((NB, NB), 0) == iota((NB, NB), 1)
    panels = ORDER // NB

    def panel(k, carry):
        here = pl.ds(pl.multiple_of(k * NB, NB), NB)
        diag = system[here, here]
        block[...] = diag
        factor_inverse(block, cols, rows16)
        inv_high, inv_low = split(block[...])
        inv_cat = jnp.concatenate([inv_high, inv_high, inv_low], axis=1)
        inv_cat2 = jnp.concatenate([inv_high, inv_low, inv_high], axis=1)
        col_high, col_low = split(system[:, here])
        col = dot_t(jnp.concatenate([col_high, col_low, col_high], axis=1), inv_cat)
        row_at = iota((ORDER, NB), 0) - k * NB
        col = jnp.where(row_at >= iota((ORDER, NB), 1), col, 0.0)
        system[:, here] = col
        low_high, low_low = split(jnp.where(row_at >= NB, col, 0.0))
        low1[...] = jnp.concatenate([low_high, low_low, low_high], axis=1)
        low2[...] = jnp.concatenate([low_high, low_high, low_low], axis=1)
        row_high, row_low = split(out_ref[here, :])
        solved = dot(inv_cat2, jnp.concatenate([row_high, row_high, row_low], axis=0))
        out_ref[here, :] = solved
        sol_high, sol_low = split(solved)
        wide[...] = jnp.concatenate([sol_high, sol_high, sol_low], axis=0)

        def trail(i, carry):
            at = pl.ds(pl.multiple_of(i * NB, NB), NB)
            rows = low1[at, :]
            out_ref[at, :] -= dot(rows, wide[...])
            system[at, :] -= dot_t(rows, low2[...])
            return carry

        lax.fori_loop(k + 1, panels, trail, 0)
        return carry

    def damped(k, carry):
        here = pl.ds(pl.multiple_of(k * NB, NB), NB)
        diag = system[here, here]
        system[here, here] = diag + jnp.where(eye, scale * (diag + 1.0), 0.0)
        return carry

    lax.fori_loop(0, panels, damped, 0)
    lax.fori_loop(0, panels, panel, 0)

    @pl.when(on_diag)
    def _():
        out_ref[...] = system[...]


def feature_order():
    order = np.zeros((FEAT, FEAT), np.float32)
    for q in range(FEAT):
        if q < 18 * OBS:
            i, rest = divmod(q, 24)
            o, r = divmod(rest, 6)
            order[q, 18 * o + 3 * r + i] = 1.0
        else:
            order[q, q] = 1.0
    return order


def feature_spread():
    wide = np.zeros((48 * OBS, 6 * OBS), np.float32)
    for row in range(48 * OBS):
        o, x = divmod(row, 48)
        wide[row, 6 * o + x % 6] = 1.0
    return wide


def solve(place_at, recv):
    total = recv.shape[0]
    vmem = pl.BlockSpec(memory_space=pltpu.VMEM)
    return pl.pallas_call(
        solve_kernel,
        out_shape=jax.ShapeDtypeStruct((ORDER, ORDER), F32),
        in_specs=[pl.BlockSpec(memory_space=pltpu.SMEM), vmem, vmem, vmem],
        out_specs=vmem,
        scratch_shapes=[
            pltpu.VMEM((ORDER, ORDER), F32),
            pltpu.VMEM((ORDER, 3 * CHUNK), BF16),
            pltpu.VMEM((ORDER, 3 * CHUNK), BF16),
            pltpu.VMEM((total // PAIR, total), BF16),
            pltpu.VMEM((total // PAIR, total), BF16),
            pltpu.VMEM((8, total), jnp.int32),
            pltpu.VMEM((NB, NB), F32),
            pltpu.VMEM((SUB, SUB, NB), F32),
            pltpu.VMEM((SUB, NB), F32),
            pltpu.VMEM((ORDER, 3 * NB), BF16),
            pltpu.VMEM((ORDER, 3 * NB), BF16),
            pltpu.VMEM((3 * NB, ORDER), BF16),
        ],
        compiler_params=pltpu.CompilerParams(vmem_limit_bytes=60 * 1024 * 1024),
        name="assemble_solve",
    )(place_at, recv, jnp.asarray(feature_order(), BF16), jnp.asarray(feature_spread(), BF16))


def pack(agents, clusters, jacobians, point_hessians, cameras, tiles):
    vmem = pl.BlockSpec(memory_space=pltpu.VMEM)
    local = tiles.shape[0]
    return pl.pallas_call(
        functools.partial(pack_kernel, agents, clusters),
        out_shape=jax.ShapeDtypeStruct((agents * clusters * PAIR, FEAT), BF16),
        in_specs=[vmem] * 4,
        out_specs=vmem,
        scratch_shapes=[pltpu.VMEM((FEAT, local), F32)],
        compiler_params=pltpu.CompilerParams(vmem_limit_bytes=32 * 1024 * 1024),
        name="pack",
    )(jacobians, point_hessians, cameras, tiles.reshape(1, local))


def per_device(jacobians, point_hessians, cameras, tiles, damping):
    agents = lax.axis_size("agent")
    clusters = lax.axis_size("cluster")
    packets = pack(agents, clusters, jacobians, point_hessians, cameras, tiles)
    packets = packets.reshape(agents * clusters, PAIR, FEAT)
    recv = lax.all_to_all(packets, ("agent", "cluster"), split_axis=0, concat_axis=0, tiled=True)
    recv = recv.reshape(agents * clusters * PAIR, FEAT)
    row = lax.axis_index("agent")
    col = lax.axis_index("cluster")
    damp = lax.dynamic_index_in_dim(damping, row, keepdims=False)
    return solve(jnp.stack([row, col, damp]).astype(jnp.int32), recv)


def solution(mesh):
    in_specs = (
        P(None, ("agent", "cluster")),
        P(None, ("agent", "cluster")),
        P(None, ("agent", "cluster")),
        P(("agent", "cluster")),
        P(),
    )
    return jax.shard_map(
        per_device, mesh=mesh, in_specs=in_specs, out_specs=P("agent", "cluster"), check_vma=False
    )
```

```python
import functools

import jax
import jax.numpy as jnp
import numpy as np
from jax import lax
from jax.experimental import pallas as pl
from jax.experimental.pallas import tpu as pltpu
from jax.sharding import PartitionSpec as P

F32 = jnp.float32
BF16 = jnp.bfloat16
CAMS = 256
OBS = 4
ORDER = 6 * CAMS
ROOM = 12
PAIR = 2 * ROOM
FEAT = 128
CHUNK = 256
NB = 128
INTERLEAVE = True
SEGMENTS = (0, 3, 6, 9, 11)
SUB = 32
PAIRED = 2


def iota(shape, dim):
    return lax.broadcasted_iota(jnp.int32, shape, dim)


def dot_t(left, right):
    return lax.dot_general(left, right, (((1,), (1,)), ((), ())), preferred_element_type=F32)


def dot(left, right):
    return jnp.dot(left, right, preferred_element_type=F32)


def split(x):
    high = x.astype(BF16)
    return high, (x - high.astype(F32)).astype(BF16)


def pack_kernel(agents, clusters, jac_ref, hess_ref, cam_ref, tile_ref, out_ref, feat):
    devices = agents * clusters
    local = tile_ref.shape[1]
    tiles = tile_ref[...]
    hot = iota((devices, local), 0) == tiles
    tri = (iota((local, local), 0) <= iota((local, local), 1)).astype(F32).astype(BF16)
    count = dot(hot.astype(F32).astype(BF16), tri)
    rank = jnp.sum(jnp.where(hot, count, 0.0), axis=0, keepdims=True) - 1.0
    key = tiles * 16 + rank.astype(jnp.int32)
    hess = hess_ref[...]
    high = hess.astype(BF16).astype(F32)
    rest = hess - high
    mid = rest.astype(BF16).astype(F32)
    feat[...] = jnp.zeros_like(feat)
    feat[0:72, :] = jac_ref[...].astype(F32)
    feat[72:78, :] = high
    feat[80:86, :] = mid
    feat[88:94, :] = rest - mid
    feat[96:100, :] = cam_ref[...].astype(F32)
    feat[100:101, :] = jnp.ones((1, local), F32)
    feats = feat[...].astype(BF16)
    slot = iota((PAIR, local), 0)
    own = slot < ROOM
    rows = clusters * PAIR

    def agent(b, carry):
        parts = []
        for d in range(clusters):
            want = jnp.where(own, (b * clusters + d) * 16 + slot, (b * clusters + b) * 16 + slot - ROOM)
            parts.append(jnp.where(want == key, 1.0, 0.0).astype(F32))
        pick = jnp.concatenate(parts, axis=0).astype(BF16)
        out_ref[pl.ds(pl.multiple_of(b * rows, rows), rows), :] = dot_t(pick, feats).astype(BF16)
        return carry

    lax.fori_loop(0, agents, agent, 0)


def factor_inverse(block, cols, rows):
    nb, group = SUB, PAIRED
    tall = nb // 8
    lane = iota((nb, NB), 1)
    sub = iota((nb, NB), 0)
    lane_all = iota((NB, NB), 1)

    def spread(x, at):
        return jnp.broadcast_to(x[at : at + 1, :], (8, NB))

    for k in range(NB // nb):
        o = nb * k
        x = block[o : o + nb, :]
        for j in range(nb):
            cols[j] = jnp.broadcast_to(x[:, o + j : o + j + 1], (nb, NB))
        yield
        inside = (lane >= o) & (lane < o + nb)
        start = jnp.where(inside, jnp.where(lane - o == sub, 1.0, 0.0).astype(F32), x)
        col = [[cols[j, 8 * h : 8 * h + 8, :] for h in range(tall)] for j in range(nb)]
        row = [start[8 * h : 8 * h + 8, :] for h in range(tall)]
        for j in range(0, nb, group):
            first = j // 8
            ends = (j + group) % 8 == 0
            s = [[spread(col[j + c][first], (j + a) % 8) if c <= a else None for c in range(group)] for a in range(group)]
            low = [[None] * group for _ in range(group)]
            root = [None] * group
            for c in range(group):
                root[c] = lax.rsqrt(s[c][c])
                for a in range(c + 1, group):
                    low[a][c] = s[a][c] * root[c]
                for a in range(c + 1, group):
                    for e in range(c + 1, a + 1):
                        s[a][e] = s[a][e] - low[a][c] * low[e][c]
            under = [[None] * tall for _ in range(group)]
            done = [None] * group
            for c in range(group):
                for h in range(first + ends, tall):
                    part = col[j + c][h]
                    for e in range(c):
                        part = part - under[e][h] * low[c][e]
                    under[c][h] = part * root[c]
                part = spread(row[first], (j + c) % 8)
                for e in range(c):
                    part = part - done[e] * low[c][e]
                done[c] = part * root[c]
                rows[j + c : j + c + 1, :] = done[c][0:1, :]
            for q in range(j + group, nb):
                by = [spread(under[c][q // 8], q % 8) for c in range(group)]
                for h in range(q // 8, tall):
                    for c in range(group):
                        col[q][h] = col[q][h] - under[c][h] * by[c]
            for h in range(first + ends, tall):
                for c in range(group):
                    row[h] = row[h] - under[c][h] * done[c]
            if ends:
                yield
        result = rows[...]
        kept = jnp.where((lane_all >= o) & (lane_all < o + nb), 0.0, block[...])
        if k < NB // nb - 1:
            high, low_part = split(result)
            left_high, left_low = split(jnp.where(lane >= o + nb, result, 0.0))
            left = jnp.concatenate([left_high, left_high, left_low], axis=0)
            right = jnp.concatenate([high, low_part, high], axis=0)
            kept = kept - lax.dot_general(left, right, (((0,), (0,)), ((), ())), preferred_element_type=F32)
        block[...] = kept
        block[o : o + nb, :] = result
        yield


def slots_of(recv_ref, source_ref, before_ref, place_ref):
    total = recv_ref.shape[0]
    sources = total // PAIR
    flag = jnp.where(iota((8, FEAT), 1) == 100, 1.0, 0.0).astype(F32).astype(BF16)
    valid = dot_t(flag, recv_ref[...])
    lane = iota((8, total), 1).astype(F32)
    source = jnp.floor((lane + 0.5) * (1.0 / PAIR))
    slot = lane - source * PAIR
    home = iota((sources, total), 0).astype(F32)
    source_row = jnp.broadcast_to(source[0:1, :], (sources, total))
    source_ref[...] = jnp.where(home == source_row, 1.0, 0.0).astype(F32).astype(BF16)
    before_ref[...] = jnp.where(home < source_row, 1.0, 0.0).astype(F32).astype(BF16)
    counts = []
    for part in range(2):
        mine = (slot < ROOM) if part == 0 else (slot >= ROOM)
        here = jnp.where(mine, valid, 0.0)
        per_source = dot_t(here.astype(BF16), source_ref[...])
        offset = dot(per_source.astype(BF16), before_ref[...])
        place = jnp.where(here > 0.5, offset + slot - part * ROOM, -1.0)
        place_ref[part : part + 1, :] = place[0:1, :].astype(jnp.int32)
        counts.append(jnp.sum(here[0:1, :]).astype(jnp.int32))
    return counts


def assemble(diagonal, part, count, recv_ref, place_ref, order_ref, spread_ref, left, right, target):
    target[...] = jnp.zeros_like(target)
    total = recv_ref.shape[0]
    left_obs = range(OBS) if diagonal else (0, 1)
    right_obs = range(OBS) if diagonal else (2, 3)

    def chunk(at, carry):
        want = iota((CHUNK, total), 0) + at * CHUNK
        pick = jnp.where(want == place_ref[part : part + 1, :], 1.0, 0.0).astype(F32).astype(BF16)
        tracks = dot(pick, recv_ref[...]).astype(BF16)
        x = dot_t(order_ref[...], tracks)
        h = x[72:80, :] + x[80:88, :] + x[88:96, :]
        a, b, c, d, e, f = (h[q : q + 1, :] for q in range(6))
        c00 = b * c - f * f
        c11 = a * c - e * e
        c22 = a * b - d * d
        c01 = e * f - d * c
        c02 = d * f - e * b
        c12 = d * e - a * f
        det = a * c00 + d * c01 + e * c02
        det = jnp.where(x[100:101, :] > 0.5, det, 1.0)
        inv = [[c00 / det, c01 / det, c02 / det], [c01 / det, c11 / det, c12 / det], [c02 / det, c12 / det, c22 / det]]
        jac = [x[24 * i : 24 * i + 24, :] for i in range(3)]
        wide_j, wide_w = [], []
        for j in range(3):
            w = jac[0] * inv[0][j] + jac[1] * inv[1][j] + jac[2] * inv[2][j]
            wide_w.append(dot(spread_ref[...], w.astype(BF16)).astype(BF16))
            wide_j.append(dot(spread_ref[...], jac[j].astype(BF16)).astype(BF16))
        cams = [jnp.broadcast_to(x[96 + o : 97 + o, :].astype(BF16), (48, CHUNK)) for o in range(OBS)]
        local_cam = jnp.floor((iota((48, CHUNK), 0).astype(F32) + 0.5) * (1.0 / 6.0))

        def rows(q, carry):
            cam = (local_cam + (8 * q).astype(F32)).astype(BF16)
            at_row = pl.ds(pl.multiple_of(q * 48, 48), 48)
            hits = [cam == cams[o] for o in range(OBS)]
            for j in range(3):
                at_col = slice(CHUNK * j, CHUNK * (j + 1))
                for obs, wide, out in ((left_obs, wide_w[j], left), (right_obs, wide_j[j], right)):
                    value = jnp.zeros((48, CHUNK), BF16)
                    for o in obs:
                        value = jnp.where(hits[o], wide[48 * o : 48 * o + 48, :], value)
                    out[at_row, at_col] = value
            return carry

        lax.fori_loop(0, ORDER // 48, rows, 0)
        step = 256
        for m in range(ORDER // step):
            at_row = slice(step * m, step * (m + 1))
            if diagonal:
                upto = slice(0, step * (m + 1))
                both = dot_t(left[at_row, :], right[upto, :]) + dot_t(right[at_row, :], left[upto, :])
                target[at_row, upto] += 0.5 * both
            else:
                target[at_row, :] += dot_t(left[at_row, :], right[...])
        return carry

    lax.fori_loop(0, (count + CHUNK - 1) // CHUNK, chunk, 0)


def solve_kernel(
    place_at, recv_ref, order_ref, spread_ref, out_ref,
    system, left, right, source, before, place, block, cols, rows, low1, low2, wide,
):
    b, d, damp = place_at[0], place_at[1], place_at[2]
    on_diag = b == d
    own_count, diag_count = slots_of(recv_ref, source, before, place)
    own_count = jnp.where(on_diag, 0, own_count)
    assemble(False, 0, own_count, recv_ref, place, order_ref, spread_ref, left, right, out_ref)
    assemble(True, 1, diag_count, recv_ref, place, order_ref, spread_ref, left, right, system)
    scale = damp.astype(F32) / 8.0
    eye = iota((NB, NB), 0) == iota((NB, NB), 1)
    panels = ORDER // NB

    def work(first, k):
        here = pl.ds(pl.multiple_of(k * NB, NB), NB)
        base = first * NB
        inv_high, inv_low = split(block[...])
        inv_cat = jnp.concatenate([inv_high, inv_high, inv_low], axis=1)
        inv_cat2 = jnp.concatenate([inv_high, inv_low, inv_high], axis=1)
        tasks = []

        def column():
            rows = ORDER - base
            col_high, col_low = split(system[base:, here])
            col = dot_t(jnp.concatenate([col_high, col_low, col_high], axis=1), inv_cat)
            row_at = iota((rows, NB), 0) - (k - first) * NB
            col = jnp.where(row_at >= iota((rows, NB), 1), col, 0.0)
            system[base:, here] = col
            low_high, low_low = split(jnp.where(row_at >= NB, col, 0.0))
            low1[base:, :] = jnp.concatenate([low_high, low_low, low_high], axis=1)
            low2[base:, :] = jnp.concatenate([low_high, low_high, low_low], axis=1)

        def solved(c):
            def run():
                row_high, row_low = split(out_ref[here, c])
                part = dot(inv_cat2, jnp.concatenate([row_high, row_high, row_low], axis=0))
                out_ref[here, c] = part
                sol_high, sol_low = split(part)
                wide[:, c] = jnp.concatenate([sol_high, sol_high, sol_low], axis=0)
            return run

        def trail_own(c):
            def run():
                out_ref[base + NB :, c] -= dot(low1[base + NB :, :], wide[:, c])
            return run

        def trail_system(start, stop):
            def run():
                system[start:, start:stop] -= dot_t(low1[start:, :], low2[start:stop, :])
            return run

        tasks.append(column)
        step = 512
        for c in range(0, ORDER, step):
            tasks.append(solved(slice(c, c + step)))
        if base + NB == ORDER:
            return tasks
        step = 256
        for c in range(0, ORDER, step):
            tasks.append(trail_own(slice(c, c + step)))
        for c in range(base + NB, ORDER, step):
            tasks.append(trail_system(c, min(c + step, ORDER)))
        return tasks

    def next_block(k):
        here = pl.ds(pl.multiple_of(k * NB, NB), NB)
        after = pl.ds(pl.multiple_of((k + 1) * NB, NB), NB)
        inv_high, inv_low = split(block[...])
        low_high, low_low = split(system[after, here])
        low = dot_t(
            jnp.concatenate([low_high, low_low, low_high], axis=1),
            jnp.concatenate([inv_high, inv_high, inv_low], axis=1),
        )
        low_high, low_low = split(low)
        gram = dot_t(
            jnp.concatenate([low_high, low_low, low_high], axis=1),
            jnp.concatenate([low_high, low_high, low_low], axis=1),
        )
        return system[after, after] - gram

    def interleave(chain, tasks, steps):
        given = 0
        for at, _ in enumerate(chain):
            until = min(len(tasks), (at + 1) * len(tasks) // steps + 1) if INTERLEAVE else 0
            while given < until:
                tasks[given]()
                given += 1
        for task in tasks[given:]:
            task()

    def segment(first, last):
        def panel(k, carry):
            tasks = work(first, k)
            block[...] = next_block(k)
            interleave(factor_inverse(block, cols, rows), tasks, (2 + SUB // 8) * (NB // SUB))
            return carry

        lax.fori_loop(first, last, panel, 0)

    def damped(k, carry):
        here = pl.ds(pl.multiple_of(k * NB, NB), NB)
        diag = system[here, here]
        system[here, here] = diag + jnp.where(eye, scale * (diag + 1.0), 0.0)
        return carry

    lax.fori_loop(0, panels, damped, 0)
    block[...] = system[0:NB, 0:NB]
    for _ in factor_inverse(block, cols, rows):
        pass
    for first, last in zip(SEGMENTS[:-1], SEGMENTS[1:]):
        segment(first, last)
    for task in work(panels - 1, panels - 1):
        task()

    @pl.when(on_diag)
    def _():
        def lower(k, carry):
            at = pl.ds(pl.multiple_of(k * NB, NB), NB)
            keep = iota((NB, ORDER), 0) + k * NB >= iota((NB, ORDER), 1)
            out_ref[at, :] = jnp.where(keep, system[at, :], 0.0)
            return carry

        lax.fori_loop(0, panels, lower, 0)


def feature_order():
    order = np.zeros((FEAT, FEAT), np.float32)
    for q in range(FEAT):
        if q < 18 * OBS:
            i, rest = divmod(q, 24)
            o, r = divmod(rest, 6)
            order[q, 18 * o + 3 * r + i] = 1.0
        else:
            order[q, q] = 1.0
    return order


def feature_spread():
    wide = np.zeros((48 * OBS, 6 * OBS), np.float32)
    for row in range(48 * OBS):
        o, x = divmod(row, 48)
        wide[row, 6 * o + x % 6] = 1.0
    return wide


def solve(place_at, recv):
    total = recv.shape[0]
    vmem = pl.BlockSpec(memory_space=pltpu.VMEM)
    return pl.pallas_call(
        solve_kernel,
        out_shape=jax.ShapeDtypeStruct((ORDER, ORDER), F32),
        in_specs=[pl.BlockSpec(memory_space=pltpu.SMEM), vmem, vmem, vmem],
        out_specs=vmem,
        scratch_shapes=[
            pltpu.VMEM((ORDER, ORDER), F32),
            pltpu.VMEM((ORDER, 3 * CHUNK), BF16),
            pltpu.VMEM((ORDER, 3 * CHUNK), BF16),
            pltpu.VMEM((total // PAIR, total), BF16),
            pltpu.VMEM((total // PAIR, total), BF16),
            pltpu.VMEM((8, total), jnp.int32),
            pltpu.VMEM((NB, NB), F32),
            pltpu.VMEM((SUB, SUB, NB), F32),
            pltpu.VMEM((SUB, NB), F32),
            pltpu.VMEM((ORDER, 3 * NB), BF16),
            pltpu.VMEM((ORDER, 3 * NB), BF16),
            pltpu.VMEM((3 * NB, ORDER), BF16),
        ],
        compiler_params=pltpu.CompilerParams(vmem_limit_bytes=60 * 1024 * 1024),
        name="assemble_solve",
    )(place_at, recv, jnp.asarray(feature_order(), BF16), jnp.asarray(feature_spread(), BF16))


def pack(agents, clusters, jacobians, point_hessians, cameras, tiles):
    vmem = pl.BlockSpec(memory_space=pltpu.VMEM)
    local = tiles.shape[0]
    return pl.pallas_call(
        functools.partial(pack_kernel, agents, clusters),
        out_shape=jax.ShapeDtypeStruct((agents * clusters * PAIR, FEAT), BF16),
        in_specs=[vmem] * 4,
        out_specs=vmem,
        scratch_shapes=[pltpu.VMEM((FEAT, local), F32)],
        compiler_params=pltpu.CompilerParams(vmem_limit_bytes=32 * 1024 * 1024),
        name="pack",
    )(jacobians, point_hessians, cameras, tiles.reshape(1, local))


def per_device(jacobians, point_hessians, cameras, tiles, damping):
    agents = lax.axis_size("agent")
    clusters = lax.axis_size("cluster")
    packets = pack(agents, clusters, jacobians, point_hessians, cameras, tiles)
    packets = packets.reshape(agents * clusters, PAIR, FEAT)
    recv = lax.all_to_all(packets, ("agent", "cluster"), split_axis=0, concat_axis=0, tiled=True)
    recv = recv.reshape(agents * clusters * PAIR, FEAT)
    row = lax.axis_index("agent")
    col = lax.axis_index("cluster")
    damp = lax.dynamic_index_in_dim(damping, row, keepdims=False)
    return solve(jnp.stack([row, col, damp]).astype(jnp.int32), recv)


def solution(mesh):
    in_specs = (
        P(None, ("agent", "cluster")),
        P(None, ("agent", "cluster")),
        P(None, ("agent", "cluster")),
        P(("agent", "cluster")),
        P(),
    )
    return jax.shard_map(
        per_device, mesh=mesh, in_specs=in_specs, out_specs=P("agent", "cluster"), check_vma=False
    )
```

```python
import functools

import jax
import jax.numpy as jnp
import numpy as np
from jax import lax
from jax.experimental import pallas as pl
from jax.experimental.pallas import tpu as pltpu
from jax.sharding import PartitionSpec as P

F32 = jnp.float32
BF16 = jnp.bfloat16
CAMS = 256
OBS = 4
ORDER = 6 * CAMS
ROOM = 12
PAIR = 2 * ROOM
FEAT = 128
CHUNK = 256
NB = 128
SEGMENTS = (0, 3, 5)
SUB = 32
SHARED = 24
PAIRED = 2


def iota(shape, dim):
    return lax.broadcasted_iota(jnp.int32, shape, dim)


def dot_t(left, right):
    return lax.dot_general(left, right, (((1,), (1,)), ((), ())), preferred_element_type=F32)


def dot(left, right):
    return jnp.dot(left, right, preferred_element_type=F32)


def split(x):
    high = x.astype(BF16)
    return high, (x - high.astype(F32)).astype(BF16)


def pack_kernel(agents, clusters, jac_ref, hess_ref, cam_ref, tile_ref, out_ref, feat):
    devices = agents * clusters
    local = tile_ref.shape[1]
    tiles = tile_ref[...]
    hot = iota((devices, local), 0) == tiles
    tri = (iota((local, local), 0) <= iota((local, local), 1)).astype(F32).astype(BF16)
    count = dot(hot.astype(F32).astype(BF16), tri)
    rank = jnp.sum(jnp.where(hot, count, 0.0), axis=0, keepdims=True) - 1.0
    key = tiles * 16 + rank.astype(jnp.int32)
    hess = hess_ref[...]
    high = hess.astype(BF16).astype(F32)
    rest = hess - high
    mid = rest.astype(BF16).astype(F32)
    feat[...] = jnp.zeros_like(feat)
    feat[0:72, :] = jac_ref[...].astype(F32)
    feat[72:78, :] = high
    feat[80:86, :] = mid
    feat[88:94, :] = rest - mid
    feat[96:100, :] = cam_ref[...].astype(F32)
    feat[100:101, :] = jnp.ones((1, local), F32)
    feats = feat[...].astype(BF16)
    slot = iota((PAIR, local), 0)
    own = slot < ROOM
    rows = clusters * PAIR

    def agent(b, carry):
        parts = []
        for d in range(clusters):
            want = jnp.where(own, (b * clusters + d) * 16 + slot, (b * clusters + b) * 16 + slot - ROOM)
            parts.append(jnp.where(want == key, 1.0, 0.0).astype(F32))
        pick = jnp.concatenate(parts, axis=0).astype(BF16)
        out_ref[pl.ds(pl.multiple_of(b * rows, rows), rows), :] = dot_t(pick, feats).astype(BF16)
        return carry

    lax.fori_loop(0, agents, agent, 0)


def factor_inverse(block, cols, rows):
    nb, group = SUB, PAIRED
    tall = nb // 8
    lane = iota((nb, NB), 1)
    sub = iota((nb, NB), 0)
    lane_all = iota((NB, NB), 1)

    def spread(x, at):
        return jnp.broadcast_to(x[at : at + 1, :], (8, NB))

    for k in range(NB // nb):
        o = nb * k
        x = block[o : o + nb, :]
        for j in range(nb):
            cols[j] = jnp.broadcast_to(x[:, o + j : o + j + 1], (nb, NB))
        inside = (lane >= o) & (lane < o + nb)
        start = jnp.where(inside, jnp.where(lane - o == sub, 1.0, 0.0).astype(F32), x)
        col = [[cols[j, 8 * h : 8 * h + 8, :] for h in range(tall)] for j in range(nb)]
        row = [start[8 * h : 8 * h + 8, :] for h in range(tall)]
        for j in range(0, nb, group):
            first = j // 8
            ends = (j + group) % 8 == 0
            s = [[spread(col[j + c][first], (j + a) % 8) if c <= a else None for c in range(group)] for a in range(group)]
            low = [[None] * group for _ in range(group)]
            root = [None] * group
            for c in range(group):
                root[c] = lax.rsqrt(s[c][c])
                for a in range(c + 1, group):
                    low[a][c] = s[a][c] * root[c]
                for a in range(c + 1, group):
                    for e in range(c + 1, a + 1):
                        s[a][e] = s[a][e] - low[a][c] * low[e][c]
            under = [[None] * tall for _ in range(group)]
            done = [None] * group
            for c in range(group):
                for h in range(first + ends, tall):
                    part = col[j + c][h]
                    for e in range(c):
                        part = part - under[e][h] * low[c][e]
                    under[c][h] = part * root[c]
                part = spread(row[first], (j + c) % 8)
                for e in range(c):
                    part = part - done[e] * low[c][e]
                done[c] = part * root[c]
                rows[j + c : j + c + 1, :] = done[c][0:1, :]
            for q in range(j + group, nb):
                by = [spread(under[c][q // 8], q % 8) for c in range(group)]
                for h in range(q // 8, tall):
                    for c in range(group):
                        col[q][h] = col[q][h] - under[c][h] * by[c]
            for h in range(first + ends, tall):
                for c in range(group):
                    row[h] = row[h] - under[c][h] * done[c]
            if j < SHARED:
                yield
        result = rows[...]
        kept = jnp.where((lane_all >= o) & (lane_all < o + nb), 0.0, block[...])
        if k < NB // nb - 1:
            high, low_part = split(result)
            left_high, left_low = split(jnp.where(lane >= o + nb, result, 0.0))
            left = jnp.concatenate([left_high, left_high, left_low], axis=0)
            right = jnp.concatenate([high, low_part, high], axis=0)
            kept = kept - lax.dot_general(left, right, (((0,), (0,)), ((), ())), preferred_element_type=F32)
        block[...] = kept
        block[o : o + nb, :] = result


def slots_of(recv_ref, source_ref, before_ref, place_ref):
    total = recv_ref.shape[0]
    sources = total // PAIR
    flag = jnp.where(iota((8, FEAT), 1) == 100, 1.0, 0.0).astype(F32).astype(BF16)
    valid = dot_t(flag, recv_ref[...])
    lane = iota((8, total), 1).astype(F32)
    source = jnp.floor((lane + 0.5) * (1.0 / PAIR))
    slot = lane - source * PAIR
    home = iota((sources, total), 0).astype(F32)
    source_row = jnp.broadcast_to(source[0:1, :], (sources, total))
    source_ref[...] = jnp.where(home == source_row, 1.0, 0.0).astype(F32).astype(BF16)
    before_ref[...] = jnp.where(home < source_row, 1.0, 0.0).astype(F32).astype(BF16)
    counts = []
    for part in range(2):
        mine = (slot < ROOM) if part == 0 else (slot >= ROOM)
        here = jnp.where(mine, valid, 0.0)
        per_source = dot_t(here.astype(BF16), source_ref[...])
        offset = dot(per_source.astype(BF16), before_ref[...])
        place = jnp.where(here > 0.5, offset + slot - part * ROOM, -1.0)
        place_ref[part : part + 1, :] = place[0:1, :].astype(jnp.int32)
        counts.append(jnp.sum(here[0:1, :]).astype(jnp.int32))
    return counts


def merged(one, two):
    out, given = [], 0
    for at, step in enumerate(one):
        until = (at + 1) * len(two) // max(len(one), 1)
        out.append(step)
        out.extend(two[given:until])
        given = until
    return out + list(two[given:])


def chunk_steps(diagonal, part, at, fresh, recv_ref, place_ref, order_ref, spread_ref, left, right, target):
    total = recv_ref.shape[0]
    left_obs = range(OBS) if diagonal else (0, 1)
    right_obs = range(OBS) if diagonal else (2, 3)
    held = {}

    def select():
        want = iota((CHUNK, total), 0) + at * CHUNK
        pick = jnp.where(want == place_ref[part : part + 1, :], 1.0, 0.0).astype(F32).astype(BF16)
        tracks = dot(pick, recv_ref[...]).astype(BF16)
        held["x"] = dot_t(order_ref[...], tracks)

    def weigh():
        x = held["x"]
        h = x[72:80, :] + x[80:88, :] + x[88:96, :]
        a, b, c, d, e, f = (h[q : q + 1, :] for q in range(6))
        c00 = b * c - f * f
        c11 = a * c - e * e
        c22 = a * b - d * d
        c01 = e * f - d * c
        c02 = d * f - e * b
        c12 = d * e - a * f
        det = a * c00 + d * c01 + e * c02
        det = jnp.where(x[100:101, :] > 0.5, det, 1.0)
        inv = [[c00 / det, c01 / det, c02 / det], [c01 / det, c11 / det, c12 / det], [c02 / det, c12 / det, c22 / det]]
        jac = [x[24 * i : 24 * i + 24, :] for i in range(3)]
        held["j"], held["w"] = [], []
        for j in range(3):
            w = jac[0] * inv[0][j] + jac[1] * inv[1][j] + jac[2] * inv[2][j]
            held["w"].append(dot(spread_ref[...], w.astype(BF16)).astype(BF16))
            held["j"].append(dot(spread_ref[...], jac[j].astype(BF16)).astype(BF16))
        held["cams"] = [jnp.broadcast_to(x[96 + o : 97 + o, :].astype(BF16), (48, CHUNK)) for o in range(OBS)]
        held["local"] = jnp.floor((iota((48, CHUNK), 0).astype(F32) + 0.5) * (1.0 / 6.0)).astype(BF16)

    def rows(q):
        def run():
            cam = held["local"] + jnp.asarray(8.0 * q, BF16)
            hits = [cam == held["cams"][o] for o in range(OBS)]
            for j in range(3):
                at_col = slice(CHUNK * j, CHUNK * (j + 1))
                for obs, wide, out in ((left_obs, held["w"][j], left), (right_obs, held["j"][j], right)):
                    value = jnp.zeros((48, CHUNK), BF16)
                    for o in obs:
                        value = jnp.where(hits[o], wide[48 * o : 48 * o + 48, :], value)
                    out[48 * q : 48 * q + 48, at_col] = value
        return run

    step = 256

    def add(col, pair, row=0):
        def run():
            r = slice(step * col, ORDER) if diagonal else slice(step * row, step * (row + 1))
            c = slice(step * col, step * (col + 1))
            if diagonal:
                value = 0.5 * (dot_t(right[r, :], left[c, :]) if pair else dot_t(left[r, :], right[c, :]))
            else:
                value = dot_t(left[r, :], right[c, :])
            target[r, c] = value if fresh and not pair else target[r, c] + value
        return run

    steps = [select, weigh]
    if not diagonal:
        return steps + [rows(q) for q in range(ORDER // 48)] + [
            add(c, 0, r) for c in range(ORDER // step) for r in range(ORDER // step)
        ]
    products, ready = [], ORDER // 48
    for c in reversed(range(ORDER // step)):
        need = step * c // 48
        steps += merged([rows(q) for q in reversed(range(need, ready))], products)
        ready = need
        products = [add(c, 0), add(c, 1)]
    return steps + products


def assemble(diagonal, part, count, *refs):
    for step in chunk_steps(diagonal, part, 0, True, *refs):
        step()

    def chunk(at, carry):
        for step in chunk_steps(diagonal, part, at, False, *refs):
            step()
        return carry

    lax.fori_loop(1, (count + CHUNK - 1) // CHUNK, chunk, 0)


def solve_kernel(
    place_at, recv_ref, order_ref, spread_ref, out_ref,
    system, left, right, source, before, place, block, cols, rows, low1, low2, low3, wide, inverses,
):
    b, d, damp = place_at[0], place_at[1], place_at[2]
    on_diag = b == d
    own_count, diag_count = slots_of(recv_ref, source, before, place)
    own_count = jnp.where(on_diag, 0, own_count)
    assemble(True, 1, diag_count, recv_ref, place, order_ref, spread_ref, left, right, system)
    scale = damp.astype(F32) / 8.0
    eye = iota((NB, NB), 0) == iota((NB, NB), 1)
    panels = ORDER // NB

    def work(first, k):
        here = pl.ds(pl.multiple_of(k * NB, NB), NB)
        base = first * NB
        inv_high, inv_low = split(block[...])
        inv_cat = jnp.concatenate([inv_high, inv_high, inv_low], axis=1)

        def column():
            rows = ORDER - base
            col_high, col_low = split(system[base:, here])
            col = dot_t(jnp.concatenate([col_high, col_low, col_high], axis=1), inv_cat)
            row_at = iota((rows, NB), 0) - (k - first) * NB
            col = jnp.where(row_at >= iota((rows, NB), 1), col, 0.0)
            system[base:, here] = col
            low_high, low_low = split(jnp.where(row_at >= NB, col, 0.0))
            low1[base:, :] = jnp.concatenate([low_high, low_low, low_high], axis=1)
            low2[base:, :] = jnp.concatenate([low_high, low_high, low_low], axis=1)

        def trail(row, start, stop):
            def run():
                at = slice(row, min(row + 512, ORDER))
                system[at, start:stop] -= dot_t(low1[at, :], low2[start:stop, :])
            return run

        step = 256
        return [column] + [
            trail(r, c, min(c + step, ORDER)) for c in range(base + NB, ORDER, step) for r in range(c, ORDER, 512)
        ]

    def own_pair(p):
        at = 2 * NB * p
        mid, end = at + NB, at + 2 * NB
        held = {}

        def three(x, y):
            x_high, x_low = split(x)
            y_high, y_low = split(y)
            return dot(
                jnp.concatenate([x_high, x_low, x_high], axis=1), jnp.concatenate([y_high, y_high, y_low], axis=0)
            )

        def inverse():
            inv_a, inv_b = inverses[at:mid, :], inverses[mid:end, :]
            cross = -three(inv_b, three(system[mid:end, at:mid], inv_a))
            zero = jnp.zeros((NB, NB), F32)
            pair = jnp.concatenate(
                [jnp.concatenate([inv_a, zero], axis=1), jnp.concatenate([cross, inv_b], axis=1)], axis=0
            )
            high, low = split(pair)
            held["inv"] = jnp.concatenate([high, low, high], axis=1)

        def below():
            high, low = split(system[end:, at:end])
            low3[end:, :] = jnp.concatenate([high, low, high], axis=1)

        def solved(c):
            def run():
                high, low = split(out_ref[at:end, c])
                part = dot(held["inv"], jnp.concatenate([high, high, low], axis=0))
                out_ref[at:end, c] = part
                high, low = split(part)
                wide[:, c] = jnp.concatenate([high, high, low], axis=0)
            return run

        def trail(c, r):
            def run():
                out_ref[r, c] -= dot(low3[r, :], wide[:, c])
            return run

        pieces = [slice(c, c + 256) for c in range(0, ORDER, 256)]
        steps = [inverse] + [solved(c) for c in pieces]
        return steps + [below] + [trail(c, r) for c in pieces for r in pieces[p + 1 :]] if end < ORDER else steps

    def next_block(k):
        here = pl.ds(pl.multiple_of(k * NB, NB), NB)
        after = pl.ds(pl.multiple_of((k + 1) * NB, NB), NB)
        inv_high, inv_low = split(block[...])
        low_high, low_low = split(system[after, here])
        low = dot_t(
            jnp.concatenate([low_high, low_low, low_high], axis=1),
            jnp.concatenate([inv_high, inv_high, inv_low], axis=1),
        )
        low_high, low_low = split(low)
        gram = dot_t(
            jnp.concatenate([low_high, low_low, low_high], axis=1),
            jnp.concatenate([low_high, low_high, low_low], axis=1),
        )
        return system[after, after] - gram

    def interleave(chain, tasks, steps):
        given = 0
        for at, _ in enumerate(chain):
            until = min(len(tasks), (at + 1) * len(tasks) // steps + 1)
            while given < until:
                tasks[given]()
                given += 1
        for task in tasks[given:]:
            task()

    def own_chunk(at, fresh):
        return chunk_steps(False, 0, at, fresh, recv_ref, place, order_ref, spread_ref, left, right, out_ref)

    def advance(k, tasks):
        block[...] = next_block(k)
        interleave(factor_inverse(block, cols, rows), tasks, (SHARED // PAIRED) * (NB // SUB))
        inverses[pl.ds(pl.multiple_of((k + 1) * NB, NB), NB), :] = block[...]

    def early(first, last):
        def panel(k, carry):
            more = (k + 1) * CHUNK < own_count

            @pl.when(more)
            def _():
                tasks = work(first, k)
                advance(k, merged(own_chunk(k + 1, False), tasks))

            @pl.when(jnp.logical_not(more))
            def _():
                advance(k, work(first, k))

            return carry

        lax.fori_loop(first, last, panel, 0)

    def damped(k, carry):
        here = pl.ds(pl.multiple_of(k * NB, NB), NB)
        diag = system[here, here]
        system[here, here] = diag + jnp.where(eye, scale * (diag + 1.0), 0.0)
        return carry

    lax.fori_loop(0, panels, damped, 0)
    block[...] = system[0:NB, 0:NB]
    interleave(factor_inverse(block, cols, rows), own_chunk(0, True), (SHARED // PAIRED) * (NB // SUB))
    inverses[0:NB, :] = block[...]
    for first, last in zip(SEGMENTS[:-1], SEGMENTS[1:]):
        early(first, last)
    for k in range(SEGMENTS[-1], panels - 1):
        p = k - SEGMENTS[-1]
        advance(k, merged(own_pair(p), work(k, k)) if p < panels // 2 - 1 else work(k, k))
    for task in work(panels - 1, panels - 1) + own_pair(panels // 2 - 1):
        task()

    @pl.when(on_diag)
    def _():
        def lower(k, carry):
            at = pl.ds(pl.multiple_of(k * NB, NB), NB)
            keep = iota((NB, ORDER), 0) + k * NB >= iota((NB, ORDER), 1)
            out_ref[at, :] = jnp.where(keep, system[at, :], 0.0)
            return carry

        lax.fori_loop(0, panels, lower, 0)


def feature_order():
    order = np.zeros((FEAT, FEAT), np.float32)
    for q in range(FEAT):
        if q < 18 * OBS:
            i, rest = divmod(q, 24)
            o, r = divmod(rest, 6)
            order[q, 18 * o + 3 * r + i] = 1.0
        else:
            order[q, q] = 1.0
    return order


def feature_spread():
    wide = np.zeros((48 * OBS, 6 * OBS), np.float32)
    for row in range(48 * OBS):
        o, x = divmod(row, 48)
        wide[row, 6 * o + x % 6] = 1.0
    return wide


def solve(place_at, recv):
    total = recv.shape[0]
    vmem = pl.BlockSpec(memory_space=pltpu.VMEM)
    return pl.pallas_call(
        solve_kernel,
        out_shape=jax.ShapeDtypeStruct((ORDER, ORDER), F32),
        in_specs=[pl.BlockSpec(memory_space=pltpu.SMEM), vmem, vmem, vmem],
        out_specs=vmem,
        scratch_shapes=[
            pltpu.VMEM((ORDER, ORDER), F32),
            pltpu.VMEM((ORDER, 3 * CHUNK), BF16),
            pltpu.VMEM((ORDER, 3 * CHUNK), BF16),
            pltpu.VMEM((total // PAIR, total), BF16),
            pltpu.VMEM((total // PAIR, total), BF16),
            pltpu.VMEM((8, total), jnp.int32),
            pltpu.VMEM((NB, NB), F32),
            pltpu.VMEM((SUB, SUB, NB), F32),
            pltpu.VMEM((SUB, NB), F32),
            pltpu.VMEM((ORDER, 3 * NB), BF16),
            pltpu.VMEM((ORDER, 3 * NB), BF16),
            pltpu.VMEM((ORDER, 6 * NB), BF16),
            pltpu.VMEM((6 * NB, ORDER), BF16),
            pltpu.VMEM((ORDER, NB), F32),
        ],
        compiler_params=pltpu.CompilerParams(vmem_limit_bytes=60 * 1024 * 1024),
        name="assemble_solve",
    )(place_at, recv, jnp.asarray(feature_order(), BF16), jnp.asarray(feature_spread(), BF16))


def pack(agents, clusters, jacobians, point_hessians, cameras, tiles):
    vmem = pl.BlockSpec(memory_space=pltpu.VMEM)
    local = tiles.shape[0]
    return pl.pallas_call(
        functools.partial(pack_kernel, agents, clusters),
        out_shape=jax.ShapeDtypeStruct((agents * clusters * PAIR, FEAT), BF16),
        in_specs=[vmem] * 4,
        out_specs=vmem,
        scratch_shapes=[pltpu.VMEM((FEAT, local), F32)],
        compiler_params=pltpu.CompilerParams(vmem_limit_bytes=32 * 1024 * 1024),
        name="pack",
    )(jacobians, point_hessians, cameras, tiles.reshape(1, local))


def per_device(jacobians, point_hessians, cameras, tiles, damping):
    agents = lax.axis_size("agent")
    clusters = lax.axis_size("cluster")
    packets = pack(agents, clusters, jacobians, point_hessians, cameras, tiles)
    packets = packets.reshape(agents * clusters, PAIR, FEAT)
    recv = lax.all_to_all(packets, ("agent", "cluster"), split_axis=0, concat_axis=0, tiled=True)
    recv = recv.reshape(agents * clusters * PAIR, FEAT)
    row = lax.axis_index("agent")
    col = lax.axis_index("cluster")
    damp = lax.dynamic_index_in_dim(damping, row, keepdims=False)
    return solve(jnp.stack([row, col, damp]).astype(jnp.int32), recv)


def solution(mesh):
    in_specs = (
        P(None, ("agent", "cluster")),
        P(None, ("agent", "cluster")),
        P(None, ("agent", "cluster")),
        P(("agent", "cluster")),
        P(),
    )
    return jax.shard_map(
        per_device, mesh=mesh, in_specs=in_specs, out_specs=P("agent", "cluster"), check_vma=False
    )
```

```python
import functools

import jax
import jax.numpy as jnp
import numpy as np
from jax import lax
from jax.experimental import pallas as pl
from jax.experimental.pallas import tpu as pltpu
from jax.sharding import PartitionSpec as P

F32 = jnp.float32
BF16 = jnp.bfloat16
CAMS = 256
OBS = 4
ORDER = 6 * CAMS
ROOM = 12
PAIR = 2 * ROOM
FEAT = 128
CHUNK = 256
NB = 128
SEGMENTS = (0, 3, 5)
SUB = 32
SHARED = 24
INNER = 16
PAIRED = 2


def iota(shape, dim):
    return lax.broadcasted_iota(jnp.int32, shape, dim)


def dot_t(left, right):
    return lax.dot_general(left, right, (((1,), (1,)), ((), ())), preferred_element_type=F32)


def dot(left, right):
    return jnp.dot(left, right, preferred_element_type=F32)


def split(x):
    high = x.astype(BF16)
    return high, (x - high.astype(F32)).astype(BF16)


def pack_kernel(agents, clusters, jac_ref, hess_ref, cam_ref, tile_ref, out_ref, feat):
    devices = agents * clusters
    local = tile_ref.shape[1]
    tiles = tile_ref[...]
    hot = iota((devices, local), 0) == tiles
    tri = (iota((local, local), 0) <= iota((local, local), 1)).astype(F32).astype(BF16)
    count = dot(hot.astype(F32).astype(BF16), tri)
    rank = jnp.sum(jnp.where(hot, count, 0.0), axis=0, keepdims=True) - 1.0
    key = tiles * 16 + rank.astype(jnp.int32)
    hess = hess_ref[...]
    high = hess.astype(BF16).astype(F32)
    rest = hess - high
    mid = rest.astype(BF16).astype(F32)
    feat[...] = jnp.zeros_like(feat)
    feat[0:72, :] = jac_ref[...].astype(F32)
    feat[72:78, :] = high
    feat[80:86, :] = mid
    feat[88:94, :] = rest - mid
    feat[96:100, :] = cam_ref[...].astype(F32)
    feat[100:101, :] = jnp.ones((1, local), F32)
    feats = feat[...].astype(BF16)
    slot = iota((PAIR, local), 0)
    own = slot < ROOM
    rows = clusters * PAIR

    def agent(b, carry):
        parts = []
        for d in range(clusters):
            want = jnp.where(own, (b * clusters + d) * 16 + slot, (b * clusters + b) * 16 + slot - ROOM)
            parts.append(jnp.where(want == key, 1.0, 0.0).astype(F32))
        pick = jnp.concatenate(parts, axis=0).astype(BF16)
        out_ref[pl.ds(pl.multiple_of(b * rows, rows), rows), :] = dot_t(pick, feats).astype(BF16)
        return carry

    lax.fori_loop(0, agents, agent, 0)


def factor_inverse(block, cols, rows):
    nb, group, inner = SUB, PAIRED, INNER
    tall = nb // 8
    lane = iota((nb, NB), 1)
    sub = iota((nb, NB), 0)
    lane8 = iota((8, NB), 1)
    sub8 = iota((8, NB), 0)
    lane_all = iota((NB, NB), 1)

    def spread(x, at):
        return jnp.broadcast_to(x[at : at + 1, :], (8, NB))

    for k in range(NB // nb):
        o = nb * k
        row = [block[o + 8 * h : o + 8 * h + 8, :] for h in range(tall)]
        for i0 in range(0, nb, inner):
            top = i0 // 8
            col = [[None] * tall for _ in range(nb)]
            for j in range(i0, i0 + inner):
                for h in range(j // 8, tall):
                    col[j][h] = jnp.broadcast_to(row[h][:, o + j : o + j + 1], (8, NB))
            inside = (lane8 >= o + i0) & (lane8 < o + i0 + inner)
            for h in range(top, tall):
                own = jnp.where(lane8 - o == sub8 + 8 * h, 1.0, 0.0).astype(F32) if h < top + inner // 8 else 0.0
                row[h] = jnp.where(inside, own, row[h])
            for j in range(i0, i0 + inner, group):
                first = j // 8
                ends = (j + group) % 8 == 0
                s = [[spread(col[j + c][first], (j + a) % 8) if c <= a else None for c in range(group)] for a in range(group)]
                low = [[None] * group for _ in range(group)]
                root = [None] * group
                for c in range(group):
                    root[c] = lax.rsqrt(s[c][c])
                    for a in range(c + 1, group):
                        low[a][c] = s[a][c] * root[c]
                    for a in range(c + 1, group):
                        for e in range(c + 1, a + 1):
                            s[a][e] = s[a][e] - low[a][c] * low[e][c]
                under = [[None] * tall for _ in range(group)]
                done = [None] * group
                for c in range(group):
                    for h in range(first + ends, tall):
                        part = col[j + c][h]
                        for e in range(c):
                            part = part - under[e][h] * low[c][e]
                        under[c][h] = part * root[c]
                    part = spread(row[first], (j + c) % 8)
                    for e in range(c):
                        part = part - done[e] * low[c][e]
                    done[c] = part * root[c]
                    rows[j + c : j + c + 1, :] = done[c][0:1, :]
                for q in range(j + group, i0 + inner):
                    by = [spread(under[c][q // 8], q % 8) for c in range(group)]
                    for h in range(q // 8, tall):
                        for c in range(group):
                            col[q][h] = col[q][h] - under[c][h] * by[c]
                for h in range(first + ends, tall):
                    for c in range(group):
                        row[h] = row[h] - under[c][h] * done[c]
                if j < SHARED:
                    yield
        result = rows[...]
        for i0 in range(0, nb - inner, inner):
            stale = (lane >= o + i0 + inner) & (lane < o + nb) & (sub >= i0) & (sub < i0 + inner)
            result = jnp.where(stale, 0.0, result)
        kept = jnp.where((lane_all >= o) & (lane_all < o + nb), 0.0, block[...])
        if k < NB // nb - 1:
            high, low_part = split(result)
            left_high, left_low = split(jnp.where(lane >= o + nb, result, 0.0))
            left = jnp.concatenate([left_high, left_high, left_low], axis=0)
            right = jnp.concatenate([high, low_part, high], axis=0)
            kept = kept - lax.dot_general(left, right, (((0,), (0,)), ((), ())), preferred_element_type=F32)
        block[...] = kept
        block[o : o + nb, :] = result


def slots_of(recv_ref, source_ref, before_ref, place_ref):
    total = recv_ref.shape[0]
    sources = total // PAIR
    flag = jnp.where(iota((8, FEAT), 1) == 100, 1.0, 0.0).astype(F32).astype(BF16)
    valid = dot_t(flag, recv_ref[...])
    lane = iota((8, total), 1).astype(F32)
    source = jnp.floor((lane + 0.5) * (1.0 / PAIR))
    slot = lane - source * PAIR
    home = iota((sources, total), 0).astype(F32)
    source_row = jnp.broadcast_to(source[0:1, :], (sources, total))
    source_ref[...] = jnp.where(home == source_row, 1.0, 0.0).astype(F32).astype(BF16)
    before_ref[...] = jnp.where(home < source_row, 1.0, 0.0).astype(F32).astype(BF16)
    counts = []
    for part in range(2):
        mine = (slot < ROOM) if part == 0 else (slot >= ROOM)
        here = jnp.where(mine, valid, 0.0)
        per_source = dot_t(here.astype(BF16), source_ref[...])
        offset = dot(per_source.astype(BF16), before_ref[...])
        place = jnp.where(here > 0.5, offset + slot - part * ROOM, -1.0)
        place_ref[part : part + 1, :] = place[0:1, :].astype(jnp.int32)
        counts.append(jnp.sum(here[0:1, :]).astype(jnp.int32))
    return counts


def merged(one, two):
    out, given = [], 0
    for at, step in enumerate(one):
        until = (at + 1) * len(two) // max(len(one), 1)
        out.append(step)
        out.extend(two[given:until])
        given = until
    return out + list(two[given:])


def chunk_steps(diagonal, part, at, fresh, recv_ref, place_ref, order_ref, spread_ref, left, right, target):
    total = recv_ref.shape[0]
    left_obs = range(OBS) if diagonal else (0, 1)
    right_obs = range(OBS) if diagonal else (2, 3)
    held = {}

    def select():
        want = iota((CHUNK, total), 0) + at * CHUNK
        pick = jnp.where(want == place_ref[part : part + 1, :], 1.0, 0.0).astype(F32).astype(BF16)
        tracks = dot(pick, recv_ref[...]).astype(BF16)
        held["x"] = dot_t(order_ref[...], tracks)

    def weigh():
        x = held["x"]
        h = x[72:80, :] + x[80:88, :] + x[88:96, :]
        a, b, c, d, e, f = (h[q : q + 1, :] for q in range(6))
        c00 = b * c - f * f
        c11 = a * c - e * e
        c22 = a * b - d * d
        c01 = e * f - d * c
        c02 = d * f - e * b
        c12 = d * e - a * f
        det = a * c00 + d * c01 + e * c02
        det = jnp.where(x[100:101, :] > 0.5, det, 1.0)
        inv = [[c00 / det, c01 / det, c02 / det], [c01 / det, c11 / det, c12 / det], [c02 / det, c12 / det, c22 / det]]
        jac = [x[24 * i : 24 * i + 24, :] for i in range(3)]
        held["j"], held["w"] = [], []
        for j in range(3):
            w = jac[0] * inv[0][j] + jac[1] * inv[1][j] + jac[2] * inv[2][j]
            held["w"].append(dot(spread_ref[...], w.astype(BF16)).astype(BF16))
            held["j"].append(dot(spread_ref[...], jac[j].astype(BF16)).astype(BF16))
        held["cams"] = [jnp.broadcast_to(x[96 + o : 97 + o, :].astype(BF16), (48, CHUNK)) for o in range(OBS)]
        held["local"] = jnp.floor((iota((48, CHUNK), 0).astype(F32) + 0.5) * (1.0 / 6.0)).astype(BF16)

    def rows(q):
        def run():
            cam = held["local"] + jnp.asarray(8.0 * q, BF16)
            hits = [cam == held["cams"][o] for o in range(OBS)]
            for j in range(3):
                at_col = slice(CHUNK * j, CHUNK * (j + 1))
                for obs, wide, out in ((left_obs, held["w"][j], left), (right_obs, held["j"][j], right)):
                    value = jnp.zeros((48, CHUNK), BF16)
                    for o in obs:
                        value = jnp.where(hits[o], wide[48 * o : 48 * o + 48, :], value)
                    out[48 * q : 48 * q + 48, at_col] = value
        return run

    step = 256

    def add(col, pair, row=0):
        def run():
            r = slice(step * col, ORDER) if diagonal else slice(step * row, step * (row + 1))
            c = slice(step * col, step * (col + 1))
            if diagonal:
                value = 0.5 * (dot_t(right[r, :], left[c, :]) if pair else dot_t(left[r, :], right[c, :]))
            else:
                value = dot_t(left[r, :], right[c, :])
            target[r, c] = value if fresh and not pair else target[r, c] + value
        return run

    if not diagonal:
        return [(select, 0.9), (weigh, 0.4)] + [(rows(q), 0.03) for q in range(ORDER // 48)] + [
            (add(c, 0, r), 0.11) for c in range(ORDER // step) for r in range(ORDER // step)
        ]
    steps = [select, weigh]
    products, ready = [], ORDER // 48
    for c in reversed(range(ORDER // step)):
        need = step * c // 48
        steps += merged([rows(q) for q in reversed(range(need, ready))], products)
        ready = need
        products = [add(c, 0), add(c, 1)]
    return steps + products


def assemble(diagonal, part, count, *refs):
    for step in chunk_steps(diagonal, part, 0, True, *refs):
        step()

    def chunk(at, carry):
        for step in chunk_steps(diagonal, part, at, False, *refs):
            step()
        return carry

    lax.fori_loop(1, (count + CHUNK - 1) // CHUNK, chunk, 0)


def solve_kernel(
    place_at, recv_ref, order_ref, spread_ref, out_ref,
    sent, own, system, left, right, source, before, place, block, cols, rows, low1, low2, low3, wide, inverses,
):
    b, d, damp = place_at[0], place_at[1], place_at[2]
    on_diag = b == d
    own_count, diag_count = slots_of(recv_ref, source, before, place)
    own_count = jnp.where(on_diag, 0, own_count)
    assemble(True, 1, diag_count, recv_ref, place, order_ref, spread_ref, left, right, system)
    scale = damp.astype(F32) / 8.0
    eye = iota((NB, NB), 0) == iota((NB, NB), 1)
    panels = ORDER // NB

    def work(first, k):
        here = pl.ds(pl.multiple_of(k * NB, NB), NB)
        base = first * NB
        inv_high, inv_low = split(block[...])
        inv_cat = jnp.concatenate([inv_high, inv_high, inv_low], axis=1)

        def column():
            rows = ORDER - base
            col_high, col_low = split(system[base:, here])
            col = dot_t(jnp.concatenate([col_high, col_low, col_high], axis=1), inv_cat)
            row_at = iota((rows, NB), 0) - (k - first) * NB
            col = jnp.where(row_at >= iota((rows, NB), 1), col, 0.0)
            system[base:, here] = col
            low_high, low_low = split(jnp.where(row_at >= NB, col, 0.0))
            low1[base:, :] = jnp.concatenate([low_high, low_low, low_high], axis=1)
            low2[base:, :] = jnp.concatenate([low_high, low_high, low_low], axis=1)

        def trail(row, start, stop):
            def run():
                at = slice(row, min(row + 512, ORDER))
                system[at, start:stop] -= dot_t(low1[at, :], low2[start:stop, :])
            return run

        step = 256
        return [(column, 0.3)] + [
            (trail(r, c, min(c + step, ORDER)), 0.15) for c in range(base + NB, ORDER, step) for r in range(c, ORDER, 512)
        ]

    def own_pair(p):
        at = 2 * NB * p
        mid, end = at + NB, at + 2 * NB
        held = {}

        def three(x, y):
            x_high, x_low = split(x)
            y_high, y_low = split(y)
            return dot(
                jnp.concatenate([x_high, x_low, x_high], axis=1), jnp.concatenate([y_high, y_high, y_low], axis=0)
            )

        def inverse():
            inv_a, inv_b = inverses[at:mid, :], inverses[mid:end, :]
            cross = -three(inv_b, three(system[mid:end, at:mid], inv_a))
            zero = jnp.zeros((NB, NB), F32)
            pair = jnp.concatenate(
                [jnp.concatenate([inv_a, zero], axis=1), jnp.concatenate([cross, inv_b], axis=1)], axis=0
            )
            high, low = split(pair)
            held["inv"] = jnp.concatenate([high, low, high], axis=1)

        def below():
            high, low = split(system[end:, at:end])
            low3[end:, :] = jnp.concatenate([high, low, high], axis=1)

        def solved(c):
            def run():
                high, low = split(own[at:end, c])
                part = dot(held["inv"], jnp.concatenate([high, high, low], axis=0))
                own[at:end, c] = part
                high, low = split(part)
                wide[:, c] = jnp.concatenate([high, high, low], axis=0)
            return run

        def trail(c, r):
            def run():
                own[r, c] -= dot(low3[r, :], wide[:, c])
            return run

        def send():
            pltpu.make_async_copy(own.at[at:end, :], out_ref.at[at:end, :], sent).start()

        pieces = [slice(c, c + 256) for c in range(0, ORDER, 256)]
        steps = [(inverse, 0.3)] + [(solved(c), 0.08) for c in pieces] + [(send, 0.0)]
        if end == ORDER:
            return steps
        return steps + [(below, 0.1)] + [(trail(c, r), 0.11) for c in pieces for r in pieces[p + 1 :]]

    def next_block(k):
        here = pl.ds(pl.multiple_of(k * NB, NB), NB)
        after = pl.ds(pl.multiple_of((k + 1) * NB, NB), NB)
        inv_high, inv_low = split(block[...])
        low_high, low_low = split(system[after, here])
        low = dot_t(
            jnp.concatenate([low_high, low_low, low_high], axis=1),
            jnp.concatenate([inv_high, inv_high, inv_low], axis=1),
        )
        low_high, low_low = split(low)
        gram = dot_t(
            jnp.concatenate([low_high, low_low, low_high], axis=1),
            jnp.concatenate([low_high, low_high, low_low], axis=1),
        )
        return system[after, after] - gram

    def interleave(chain, tasks, steps):
        total = sum(cost for _, cost in tasks)
        given, spent = 0, 0.0
        for at, _ in enumerate(chain):
            while given < len(tasks) and spent < total * (at + 1) / steps:
                tasks[given][0]()
                spent += tasks[given][1]
                given += 1
        for task, _ in tasks[given:]:
            task()

    def own_chunk(at, fresh):
        return chunk_steps(False, 0, at, fresh, recv_ref, place, order_ref, spread_ref, left, right, own)

    def advance(k, tasks):
        block[...] = next_block(k)
        interleave(factor_inverse(block, cols, rows), tasks, (SHARED // PAIRED) * (NB // SUB))
        inverses[pl.ds(pl.multiple_of((k + 1) * NB, NB), NB), :] = block[...]

    def pair_work(k, p):
        one, two = work(k, k), own_pair(p)
        return two[:1] + one[:1] + two[1:7] + merged(one[1:], two[7:])

    def early(first, last):
        def panel(k, carry):
            more = (k + 1) * CHUNK < own_count

            @pl.when(more)
            def _():
                tasks = work(first, k)
                chunk = own_chunk(k + 1, False)
                advance(k, tasks[:1] + chunk[:2] + merged(tasks[1:], chunk[2:]))

            @pl.when(jnp.logical_not(more))
            def _():
                advance(k, work(first, k))

            return carry

        lax.fori_loop(first, last, panel, 0)

    def damped(k, carry):
        here = pl.ds(pl.multiple_of(k * NB, NB), NB)
        diag = system[here, here]
        system[here, here] = diag + jnp.where(eye, scale * (diag + 1.0), 0.0)
        return carry

    lax.fori_loop(0, panels, damped, 0)
    block[...] = system[0:NB, 0:NB]
    interleave(factor_inverse(block, cols, rows), own_chunk(0, True), (SHARED // PAIRED) * (NB // SUB))
    inverses[0:NB, :] = block[...]
    for first, last in zip(SEGMENTS[:-1], SEGMENTS[1:]):
        early(first, last)
    for k in range(SEGMENTS[-1], panels - 1):
        p = k - SEGMENTS[-1]
        advance(k, pair_work(k, p) if p < panels // 2 - 1 else work(k, k))
    for task, _ in work(panels - 1, panels - 1) + own_pair(panels // 2 - 1):
        task()
    whole = pltpu.make_async_copy(own, out_ref, sent)
    whole.wait()

    @pl.when(on_diag)
    def _():
        def lower(k, carry):
            at = pl.ds(pl.multiple_of(k * NB, NB), NB)
            keep = iota((NB, ORDER), 0) + k * NB >= iota((NB, ORDER), 1)
            own[at, :] = jnp.where(keep, system[at, :], 0.0)
            return carry

        lax.fori_loop(0, panels, lower, 0)
        whole.start()
        whole.wait()


def feature_order():
    order = np.zeros((FEAT, FEAT), np.float32)
    for q in range(FEAT):
        if q < 18 * OBS:
            i, rest = divmod(q, 24)
            o, r = divmod(rest, 6)
            order[q, 18 * o + 3 * r + i] = 1.0
        else:
            order[q, q] = 1.0
    return order


def feature_spread():
    wide = np.zeros((48 * OBS, 6 * OBS), np.float32)
    for row in range(48 * OBS):
        o, x = divmod(row, 48)
        wide[row, 6 * o + x % 6] = 1.0
    return wide


def solve(place_at, recv):
    total = recv.shape[0]
    vmem = pl.BlockSpec(memory_space=pltpu.VMEM)
    return pl.pallas_call(
        solve_kernel,
        out_shape=jax.ShapeDtypeStruct((ORDER, ORDER), F32),
        in_specs=[pl.BlockSpec(memory_space=pltpu.SMEM), vmem, vmem, vmem],
        out_specs=pl.BlockSpec(memory_space=pl.ANY),
        scratch_shapes=[
            pltpu.SemaphoreType.DMA,
            pltpu.VMEM((ORDER, ORDER), F32),
            pltpu.VMEM((ORDER, ORDER), F32),
            pltpu.VMEM((ORDER, 3 * CHUNK), BF16),
            pltpu.VMEM((ORDER, 3 * CHUNK), BF16),
            pltpu.VMEM((total // PAIR, total), BF16),
            pltpu.VMEM((total // PAIR, total), BF16),
            pltpu.VMEM((8, total), jnp.int32),
            pltpu.VMEM((NB, NB), F32),
            pltpu.VMEM((SUB, SUB, NB), F32),
            pltpu.VMEM((SUB, NB), F32),
            pltpu.VMEM((ORDER, 3 * NB), BF16),
            pltpu.VMEM((ORDER, 3 * NB), BF16),
            pltpu.VMEM((ORDER, 6 * NB), BF16),
            pltpu.VMEM((6 * NB, ORDER), BF16),
            pltpu.VMEM((ORDER, NB), F32),
        ],
        compiler_params=pltpu.CompilerParams(vmem_limit_bytes=60 * 1024 * 1024),
        name="assemble_solve",
    )(place_at, recv, jnp.asarray(feature_order(), BF16), jnp.asarray(feature_spread(), BF16))


def pack(agents, clusters, jacobians, point_hessians, cameras, tiles):
    vmem = pl.BlockSpec(memory_space=pltpu.VMEM)
    local = tiles.shape[0]
    return pl.pallas_call(
        functools.partial(pack_kernel, agents, clusters),
        out_shape=jax.ShapeDtypeStruct((agents * clusters * PAIR, FEAT), BF16),
        in_specs=[vmem] * 4,
        out_specs=vmem,
        scratch_shapes=[pltpu.VMEM((FEAT, local), F32)],
        compiler_params=pltpu.CompilerParams(vmem_limit_bytes=60 * 1024 * 1024),
        name="pack",
    )(jacobians, point_hessians, cameras, tiles.reshape(1, local))


def per_device(jacobians, point_hessians, cameras, tiles, damping):
    agents = lax.axis_size("agent")
    clusters = lax.axis_size("cluster")
    packets = pack(agents, clusters, jacobians, point_hessians, cameras, tiles)
    packets = packets.reshape(agents * clusters, PAIR, FEAT)
    recv = lax.all_to_all(packets, ("agent", "cluster"), split_axis=0, concat_axis=0, tiled=True)
    recv = recv.reshape(agents * clusters * PAIR, FEAT)
    row = lax.axis_index("agent")
    col = lax.axis_index("cluster")
    damp = lax.dynamic_index_in_dim(damping, row, keepdims=False)
    return solve(jnp.stack([row, col, damp]).astype(jnp.int32), recv)


def solution(mesh):
    in_specs = (
        P(None, ("agent", "cluster")),
        P(None, ("agent", "cluster")),
        P(None, ("agent", "cluster")),
        P(("agent", "cluster")),
        P(),
    )
    return jax.shard_map(
        per_device, mesh=mesh, in_specs=in_specs, out_specs=P("agent", "cluster"), check_vma=False
    )
```

```python
import functools

import jax
import jax.numpy as jnp
import numpy as np
from jax import lax
from jax.experimental import pallas as pl
from jax.experimental.pallas import tpu as pltpu
from jax.sharding import PartitionSpec as P

F32 = jnp.float32
BF16 = jnp.bfloat16
CAMS = 256
OBS = 4
ORDER = 6 * CAMS
ROOM = 12
PAIR = 2 * ROOM
FEAT = 128
CHUNK = 256
NB = 128
SEGMENTS = (0, 3, 5)
SUB = 32
SHARED = 24
INNER = 16
PAIRED = 2


def iota(shape, dim):
    return lax.broadcasted_iota(jnp.int32, shape, dim)


def dot_t(left, right):
    return lax.dot_general(left, right, (((1,), (1,)), ((), ())), preferred_element_type=F32)


def dot(left, right):
    return jnp.dot(left, right, preferred_element_type=F32)


def split(x):
    high = x.astype(BF16)
    return high, (x - high.astype(F32)).astype(BF16)


def pack_kernel(agents, clusters, jac_ref, hess_ref, cam_ref, tile_ref, out_ref, feat):
    devices = agents * clusters
    local = tile_ref.shape[1]
    tiles = tile_ref[...]
    hot = iota((devices, local), 0) == tiles
    tri = (iota((local, local), 0) <= iota((local, local), 1)).astype(F32).astype(BF16)
    count = dot(hot.astype(F32).astype(BF16), tri)
    rank = jnp.sum(jnp.where(hot, count, 0.0), axis=0, keepdims=True) - 1.0
    key = tiles * 16 + rank.astype(jnp.int32)
    hess = hess_ref[...]
    high = hess.astype(BF16).astype(F32)
    rest = hess - high
    mid = rest.astype(BF16).astype(F32)
    feat[...] = jnp.zeros_like(feat)
    feat[0:72, :] = jac_ref[...].astype(F32)
    feat[72:78, :] = high
    feat[80:86, :] = mid
    feat[88:94, :] = rest - mid
    feat[96:100, :] = cam_ref[...].astype(F32)
    feat[100:101, :] = jnp.ones((1, local), F32)
    feats = feat[...].astype(BF16)
    slot = iota((PAIR, local), 0)
    own = slot < ROOM
    rows = clusters * PAIR

    def agent(b, carry):
        parts = []
        for d in range(clusters):
            want = jnp.where(own, (b * clusters + d) * 16 + slot, (b * clusters + b) * 16 + slot - ROOM)
            parts.append(jnp.where(want == key, 1.0, 0.0).astype(F32))
        pick = jnp.concatenate(parts, axis=0).astype(BF16)
        out_ref[pl.ds(pl.multiple_of(b * rows, rows), rows), :] = dot_t(pick, feats).astype(BF16)
        return carry

    lax.fori_loop(0, agents, agent, 0)


def factor_inverse(block, cols, rows):
    nb, group, inner = SUB, PAIRED, INNER
    tall = nb // 8
    lane = iota((nb, NB), 1)
    sub = iota((nb, NB), 0)
    lane8 = iota((8, NB), 1)
    sub8 = iota((8, NB), 0)
    lane_all = iota((NB, NB), 1)

    def spread(x, at):
        return jnp.broadcast_to(x[at : at + 1, :], (8, NB))

    for k in range(NB // nb):
        o = nb * k
        row = [block[o + 8 * h : o + 8 * h + 8, :] for h in range(tall)]
        for i0 in range(0, nb, inner):
            top = i0 // 8
            col = [[None] * tall for _ in range(nb)]
            for j in range(i0, i0 + inner):
                for h in range(j // 8, tall):
                    col[j][h] = jnp.broadcast_to(row[h][:, o + j : o + j + 1], (8, NB))
            inside = (lane8 >= o + i0) & (lane8 < o + i0 + inner)
            for h in range(top, tall):
                own = jnp.where(lane8 - o == sub8 + 8 * h, 1.0, 0.0).astype(F32) if h < top + inner // 8 else 0.0
                row[h] = jnp.where(inside, own, row[h])
            for j in range(i0, i0 + inner, group):
                first = j // 8
                ends = (j + group) % 8 == 0
                s = [[spread(col[j + c][first], (j + a) % 8) if c <= a else None for c in range(group)] for a in range(group)]
                low = [[None] * group for _ in range(group)]
                root = [None] * group
                for c in range(group):
                    root[c] = lax.rsqrt(s[c][c])
                    for a in range(c + 1, group):
                        low[a][c] = s[a][c] * root[c]
                    for a in range(c + 1, group):
                        for e in range(c + 1, a + 1):
                            s[a][e] = s[a][e] - low[a][c] * low[e][c]
                under = [[None] * tall for _ in range(group)]
                done = [None] * group
                for c in range(group):
                    for h in range(first + ends, tall):
                        part = col[j + c][h]
                        for e in range(c):
                            part = part - under[e][h] * low[c][e]
                        under[c][h] = part * root[c]
                    part = spread(row[first], (j + c) % 8)
                    for e in range(c):
                        part = part - done[e] * low[c][e]
                    done[c] = part * root[c]
                    rows[j + c : j + c + 1, :] = done[c][0:1, :]
                for q in range(j + group, i0 + inner):
                    by = [spread(under[c][q // 8], q % 8) for c in range(group)]
                    for h in range(q // 8, tall):
                        for c in range(group):
                            col[q][h] = col[q][h] - under[c][h] * by[c]
                for h in range(first + ends, tall):
                    for c in range(group):
                        row[h] = row[h] - under[c][h] * done[c]
                if j < SHARED:
                    yield
        result = rows[...]
        for i0 in range(0, nb - inner, inner):
            stale = (lane >= o + i0 + inner) & (lane < o + nb) & (sub >= i0) & (sub < i0 + inner)
            result = jnp.where(stale, 0.0, result)
        kept = jnp.where((lane_all >= o) & (lane_all < o + nb), 0.0, block[...])
        if k < NB // nb - 1:
            high, low_part = split(result)
            left_high, left_low = split(jnp.where(lane >= o + nb, result, 0.0))
            left = jnp.concatenate([left_high, left_high, left_low], axis=0)
            right = jnp.concatenate([high, low_part, high], axis=0)
            kept = kept - lax.dot_general(left, right, (((0,), (0,)), ((), ())), preferred_element_type=F32)
        block[...] = kept
        block[o : o + nb, :] = result


def slots_of(recv_ref, source_ref, before_ref, place_ref):
    total = recv_ref.shape[0]
    sources = total // PAIR
    flag = jnp.where(iota((8, FEAT), 1) == 100, 1.0, 0.0).astype(F32).astype(BF16)
    valid = dot_t(flag, recv_ref[...])
    lane = iota((8, total), 1).astype(F32)
    source = jnp.floor((lane + 0.5) * (1.0 / PAIR))
    slot = lane - source * PAIR
    home = iota((sources, total), 0).astype(F32)
    source_row = jnp.broadcast_to(source[0:1, :], (sources, total))
    source_ref[...] = jnp.where(home == source_row, 1.0, 0.0).astype(F32).astype(BF16)
    before_ref[...] = jnp.where(home < source_row, 1.0, 0.0).astype(F32).astype(BF16)
    counts = []
    for part in range(2):
        mine = (slot < ROOM) if part == 0 else (slot >= ROOM)
        here = jnp.where(mine, valid, 0.0)
        per_source = dot_t(here.astype(BF16), source_ref[...])
        offset = dot(per_source.astype(BF16), before_ref[...])
        place = jnp.where(here > 0.5, offset + slot - part * ROOM, -1.0)
        place_ref[part : part + 1, :] = place[0:1, :].astype(jnp.int32)
        counts.append(jnp.sum(here[0:1, :]).astype(jnp.int32))
    return counts


def merged(one, two):
    out, given = [], 0
    for at, step in enumerate(one):
        until = (at + 1) * len(two) // max(len(one), 1)
        out.append(step)
        out.extend(two[given:until])
        given = until
    return out + list(two[given:])


def chunk_steps(diagonal, part, size, start, fresh, recv_ref, place_ref, order_ref, spread_ref, left, right, target):
    total = recv_ref.shape[0]
    left_obs = range(OBS) if diagonal else (0, 1)
    right_obs = range(OBS) if diagonal else (2, 3)
    held = {}

    def select():
        want = iota((size, total), 0) + start
        pick = jnp.where(want == place_ref[part : part + 1, :], 1.0, 0.0).astype(F32).astype(BF16)
        tracks = dot(pick, recv_ref[...]).astype(BF16)
        held["x"] = dot_t(order_ref[...], tracks)

    def weigh():
        x = held["x"]
        h = x[72:80, :] + x[80:88, :] + x[88:96, :]
        a, b, c, d, e, f = (h[q : q + 1, :] for q in range(6))
        c00 = b * c - f * f
        c11 = a * c - e * e
        c22 = a * b - d * d
        c01 = e * f - d * c
        c02 = d * f - e * b
        c12 = d * e - a * f
        det = a * c00 + d * c01 + e * c02
        det = jnp.where(x[100:101, :] > 0.5, det, 1.0)
        inv = [[c00 / det, c01 / det, c02 / det], [c01 / det, c11 / det, c12 / det], [c02 / det, c12 / det, c22 / det]]
        jac = [x[24 * i : 24 * i + 24, :] for i in range(3)]
        held["j"], held["w"] = [], []
        for j in range(3):
            w = jac[0] * inv[0][j] + jac[1] * inv[1][j] + jac[2] * inv[2][j]
            held["w"].append(dot(spread_ref[...], w.astype(BF16)).astype(BF16))
            held["j"].append(dot(spread_ref[...], jac[j].astype(BF16)).astype(BF16))
        held["cams"] = [jnp.broadcast_to(x[96 + o : 97 + o, :].astype(BF16), (48, size)) for o in range(OBS)]
        held["local"] = jnp.floor((iota((48, size), 0).astype(F32) + 0.5) * (1.0 / 6.0)).astype(BF16)

    def rows(q):
        def run():
            cam = held["local"] + jnp.asarray(8.0 * q, BF16)
            hits = [cam == held["cams"][o] for o in range(OBS)]
            for j in range(3):
                at_col = slice(size * j, size * (j + 1))
                for obs, wide, out in ((left_obs, held["w"][j], left), (right_obs, held["j"][j], right)):
                    value = jnp.zeros((48, size), BF16)
                    for o in obs:
                        value = jnp.where(hits[o], wide[48 * o : 48 * o + 48, :], value)
                    out[48 * q : 48 * q + 48, at_col] = value
        return run

    step = 256
    k = slice(0, 3 * size)

    def add(col, pair, row=0):
        def run():
            r = slice(step * col, ORDER) if diagonal else slice(step * row, step * (row + 1))
            c = slice(step * col, step * (col + 1))
            if diagonal:
                value = 0.5 * (dot_t(right[r, k], left[c, k]) if pair else dot_t(left[r, k], right[c, k]))
            else:
                value = dot_t(left[r, k], right[c, k])
            target[r, c] = value if fresh and not pair else target[r, c] + value
        return run

    if not diagonal:
        return [(select, 0.9), (weigh, 0.4)] + [(rows(q), 0.03) for q in range(ORDER // 48)] + [
            (add(c, 0, r), 0.11) for c in range(ORDER // step) for r in range(ORDER // step)
        ]
    steps = [select, weigh]
    products, ready = [], ORDER // 48
    for c in reversed(range(ORDER // step)):
        need = step * c // 48
        steps += merged([rows(q) for q in reversed(range(need, ready))], products)
        ready = need
        products = [add(c, 0), add(c, 1)]
    return steps + products


def assemble(diagonal, part, count, *refs):
    for step in chunk_steps(diagonal, part, CHUNK, 0, True, *refs):
        step()
    full = jnp.maximum((count + CHUNK // 2 - 1) // CHUNK, 1)

    def chunk(at, carry):
        for step in chunk_steps(diagonal, part, CHUNK, at * CHUNK, False, *refs):
            step()
        return carry

    lax.fori_loop(1, full, chunk, 0)

    @pl.when(count > full * CHUNK)
    def _():
        for step in chunk_steps(diagonal, part, CHUNK // 2, full * CHUNK, False, *refs):
            step()


def solve_kernel(
    place_at, recv_ref, order_ref, spread_ref, out_ref,
    sent, own, system, left, right, source, before, place, block, cols, rows, low1, low2, low3, wide, inverses,
):
    b, d, damp = place_at[0], place_at[1], place_at[2]
    on_diag = b == d
    own_count, diag_count = slots_of(recv_ref, source, before, place)
    own_count = jnp.where(on_diag, 0, own_count)
    assemble(True, 1, diag_count, recv_ref, place, order_ref, spread_ref, left, right, system)
    scale = damp.astype(F32) / 8.0
    eye = iota((NB, NB), 0) == iota((NB, NB), 1)
    panels = ORDER // NB

    def work(first, k):
        here = pl.ds(pl.multiple_of(k * NB, NB), NB)
        base = first * NB
        inv_high, inv_low = split(block[...])
        inv_cat = jnp.concatenate([inv_high, inv_high, inv_low], axis=1)

        def column():
            rows = ORDER - base
            col_high, col_low = split(system[base:, here])
            col = dot_t(jnp.concatenate([col_high, col_low, col_high], axis=1), inv_cat)
            row_at = iota((rows, NB), 0) - (k - first) * NB
            col = jnp.where(row_at >= iota((rows, NB), 1), col, 0.0)
            system[base:, here] = col
            low_high, low_low = split(jnp.where(row_at >= NB, col, 0.0))
            low1[base:, :] = jnp.concatenate([low_high, low_low, low_high], axis=1)
            low2[base:, :] = jnp.concatenate([low_high, low_high, low_low], axis=1)

        def trail(row, start, stop):
            def run():
                at = slice(row, min(row + 512, ORDER))
                system[at, start:stop] -= dot_t(low1[at, :], low2[start:stop, :])
            return run

        step = 256
        return [(column, 0.3)] + [
            (trail(r, c, min(c + step, ORDER)), 0.15) for c in range(base + NB, ORDER, step) for r in range(c, ORDER, 512)
        ]

    def own_pair(p):
        at = 2 * NB * p
        mid, end = at + NB, at + 2 * NB
        held = {}

        def three(x, y):
            x_high, x_low = split(x)
            y_high, y_low = split(y)
            return dot(
                jnp.concatenate([x_high, x_low, x_high], axis=1), jnp.concatenate([y_high, y_high, y_low], axis=0)
            )

        def inverse():
            inv_a, inv_b = inverses[at:mid, :], inverses[mid:end, :]
            cross = -three(inv_b, three(system[mid:end, at:mid], inv_a))
            zero = jnp.zeros((NB, NB), F32)
            pair = jnp.concatenate(
                [jnp.concatenate([inv_a, zero], axis=1), jnp.concatenate([cross, inv_b], axis=1)], axis=0
            )
            high, low = split(pair)
            held["inv"] = jnp.concatenate([high, low, high], axis=1)

        def below():
            high, low = split(system[end:, at:end])
            low3[end:, :] = jnp.concatenate([high, low, high], axis=1)

        def solved(c):
            def run():
                high, low = split(own[at:end, c])
                part = dot(held["inv"], jnp.concatenate([high, high, low], axis=0))
                own[at:end, c] = part
                high, low = split(part)
                wide[:, c] = jnp.concatenate([high, high, low], axis=0)
            return run

        def trail(c, r):
            def run():
                own[r, c] -= dot(low3[r, :], wide[:, c])
            return run

        def send():
            pltpu.make_async_copy(own.at[at:end, :], out_ref.at[at:end, :], sent).start()

        pieces = [slice(c, c + 256) for c in range(0, ORDER, 256)]
        steps = [(inverse, 0.3)] + [(solved(c), 0.08) for c in pieces] + [(send, 0.0)]
        if end == ORDER:
            return steps
        return steps + [(below, 0.1)] + [(trail(c, r), 0.11) for c in pieces for r in pieces[p + 1 :]]

    def next_block(k):
        here = pl.ds(pl.multiple_of(k * NB, NB), NB)
        after = pl.ds(pl.multiple_of((k + 1) * NB, NB), NB)
        inv_high, inv_low = split(block[...])
        low_high, low_low = split(system[after, here])
        low = dot_t(
            jnp.concatenate([low_high, low_low, low_high], axis=1),
            jnp.concatenate([inv_high, inv_high, inv_low], axis=1),
        )
        low_high, low_low = split(low)
        gram = dot_t(
            jnp.concatenate([low_high, low_low, low_high], axis=1),
            jnp.concatenate([low_high, low_high, low_low], axis=1),
        )
        return system[after, after] - gram

    def interleave(chain, tasks, steps):
        total = sum(cost for _, cost in tasks)
        given, spent = 0, 0.0
        for at, _ in enumerate(chain):
            while given < len(tasks) and spent < total * (at + 1) / steps:
                tasks[given][0]()
                spent += tasks[given][1]
                given += 1
        for task, _ in tasks[given:]:
            task()

    def own_chunk(at, fresh):
        return chunk_steps(False, 0, CHUNK, at * CHUNK, fresh, recv_ref, place, order_ref, spread_ref, left, right, own)

    def advance(k, tasks):
        block[...] = next_block(k)
        interleave(factor_inverse(block, cols, rows), tasks, (SHARED // PAIRED) * (NB // SUB))
        inverses[pl.ds(pl.multiple_of((k + 1) * NB, NB), NB), :] = block[...]

    def pair_work(k, p):
        one, two = work(k, k), own_pair(p)
        return two[:1] + one[:1] + two[1:7] + merged(one[1:], two[7:])

    def early(first, last):
        def panel(k, carry):
            more = (k + 1) * CHUNK < own_count

            @pl.when(more)
            def _():
                tasks = work(first, k)
                chunk = own_chunk(k + 1, False)
                advance(k, tasks[:1] + chunk[:2] + merged(tasks[1:], chunk[2:]))

            @pl.when(jnp.logical_not(more))
            def _():
                advance(k, work(first, k))

            return carry

        lax.fori_loop(first, last, panel, 0)

    def damped(k, carry):
        here = pl.ds(pl.multiple_of(k * NB, NB), NB)
        diag = system[here, here]
        system[here, here] = diag + jnp.where(eye, scale * (diag + 1.0), 0.0)
        return carry

    lax.fori_loop(0, panels, damped, 0)
    block[...] = system[0:NB, 0:NB]
    interleave(factor_inverse(block, cols, rows), own_chunk(0, True), (SHARED // PAIRED) * (NB // SUB))
    inverses[0:NB, :] = block[...]
    for first, last in zip(SEGMENTS[:-1], SEGMENTS[1:]):
        early(first, last)
    for k in range(SEGMENTS[-1], panels - 1):
        p = k - SEGMENTS[-1]
        advance(k, pair_work(k, p) if p < panels // 2 - 1 else work(k, k))
    for task, _ in work(panels - 1, panels - 1) + own_pair(panels // 2 - 1):
        task()
    whole = pltpu.make_async_copy(own, out_ref, sent)
    whole.wait()

    @pl.when(on_diag)
    def _():
        def lower(k, carry):
            at = pl.ds(pl.multiple_of(k * NB, NB), NB)
            keep = iota((NB, ORDER), 0) + k * NB >= iota((NB, ORDER), 1)
            own[at, :] = jnp.where(keep, system[at, :], 0.0)
            return carry

        lax.fori_loop(0, panels, lower, 0)
        whole.start()
        whole.wait()


def feature_order():
    order = np.zeros((FEAT, FEAT), np.float32)
    for q in range(FEAT):
        if q < 18 * OBS:
            i, rest = divmod(q, 24)
            o, r = divmod(rest, 6)
            order[q, 18 * o + 3 * r + i] = 1.0
        else:
            order[q, q] = 1.0
    return order


def feature_spread():
    wide = np.zeros((48 * OBS, 6 * OBS), np.float32)
    for row in range(48 * OBS):
        o, x = divmod(row, 48)
        wide[row, 6 * o + x % 6] = 1.0
    return wide


def solve(place_at, recv):
    total = recv.shape[0]
    vmem = pl.BlockSpec(memory_space=pltpu.VMEM)
    return pl.pallas_call(
        solve_kernel,
        out_shape=jax.ShapeDtypeStruct((ORDER, ORDER), F32),
        in_specs=[pl.BlockSpec(memory_space=pltpu.SMEM), vmem, vmem, vmem],
        out_specs=pl.BlockSpec(memory_space=pl.ANY),
        scratch_shapes=[
            pltpu.SemaphoreType.DMA,
            pltpu.VMEM((ORDER, ORDER), F32),
            pltpu.VMEM((ORDER, ORDER), F32),
            pltpu.VMEM((ORDER, 3 * CHUNK), BF16),
            pltpu.VMEM((ORDER, 3 * CHUNK), BF16),
            pltpu.VMEM((total // PAIR, total), BF16),
            pltpu.VMEM((total // PAIR, total), BF16),
            pltpu.VMEM((8, total), jnp.int32),
            pltpu.VMEM((NB, NB), F32),
            pltpu.VMEM((SUB, SUB, NB), F32),
            pltpu.VMEM((SUB, NB), F32),
            pltpu.VMEM((ORDER, 3 * NB), BF16),
            pltpu.VMEM((ORDER, 3 * NB), BF16),
            pltpu.VMEM((ORDER, 6 * NB), BF16),
            pltpu.VMEM((6 * NB, ORDER), BF16),
            pltpu.VMEM((ORDER, NB), F32),
        ],
        compiler_params=pltpu.CompilerParams(vmem_limit_bytes=60 * 1024 * 1024),
        name="assemble_solve",
    )(place_at, recv, jnp.asarray(feature_order(), BF16), jnp.asarray(feature_spread(), BF16))


def pack(agents, clusters, jacobians, point_hessians, cameras, tiles):
    vmem = pl.BlockSpec(memory_space=pltpu.VMEM)
    local = tiles.shape[0]
    return pl.pallas_call(
        functools.partial(pack_kernel, agents, clusters),
        out_shape=jax.ShapeDtypeStruct((agents * clusters * PAIR, FEAT), BF16),
        in_specs=[vmem] * 4,
        out_specs=vmem,
        scratch_shapes=[pltpu.VMEM((FEAT, local), F32)],
        compiler_params=pltpu.CompilerParams(vmem_limit_bytes=60 * 1024 * 1024),
        name="pack",
    )(jacobians, point_hessians, cameras, tiles.reshape(1, local))


def per_device(jacobians, point_hessians, cameras, tiles, damping):
    agents = lax.axis_size("agent")
    clusters = lax.axis_size("cluster")
    packets = pack(agents, clusters, jacobians, point_hessians, cameras, tiles)
    packets = packets.reshape(agents * clusters, PAIR, FEAT)
    recv = lax.all_to_all(packets, ("agent", "cluster"), split_axis=0, concat_axis=0, tiled=True)
    recv = recv.reshape(agents * clusters * PAIR, FEAT)
    row = lax.axis_index("agent")
    col = lax.axis_index("cluster")
    damp = lax.dynamic_index_in_dim(damping, row, keepdims=False)
    return solve(jnp.stack([row, col, damp]).astype(jnp.int32), recv)


def solution(mesh):
    in_specs = (
        P(None, ("agent", "cluster")),
        P(None, ("agent", "cluster")),
        P(None, ("agent", "cluster")),
        P(("agent", "cluster")),
        P(),
    )
    return jax.shard_map(
        per_device, mesh=mesh, in_specs=in_specs, out_specs=P("agent", "cluster"), check_vma=False
    )
```
